128 devices in a mesh: gx: 8 (over z, core), gy: 16 (over y, x).
Axes of the slice: x: 4, y: 4, z: 4, core: 2. Of those that a mesh axis runs over, the one named last changes fastest.
Arguments:
- concentration: float32 [1024, 64, 4096], P(('gx', 'gy')), may hold values from 0.05 to 0.95
- neighbour: int32 [1024, 6], P(('gx', 'gy')), may hold values from -1 to 1023, as said below
- new_owner: int32 [1024], P(('gx', 'gy')), may hold values from -1 to 127, as said below
- new_slot: int32 [1024], P(('gx', 'gy')), may hold values from -1 to 7, as said below
Outputs:
- advanced: float32 [1024, 64, 4096], P(('gx', 'gy'))
The draws below stay inside these ranges and needn't reach their ends.
Inputs may be any that keep to these rules, and one draw needn't show every extreme that they name: Global slot = device * 8 + slot, devices numbered along gx then gy. The occupied slots of a device are its first ones, between 2 and 8 of them (some device has all 8); empty slots have no neighbours and are nobody's neighbour. The relation is symmetric: if h is beside g in direction d, g is beside h in the opposite direction. Along x a block's neighbours lie on its own device. Each device has exactly 2 blocks with a neighbour on another device in each of +y, -y, +z, -z; those of +y and -z lie on the device numbered one higher, those of -y and +z on the device numbered one lower (both counted around the last device back to device 0). `new_owner`: an occupied block stays on its device or goes to the device numbered one lower or one higher; a device hands at most 1 block to each side, and in every draw some device hands 1 to a side and some device receives 1 from both sides. Blocks keep their order along the curve. -1 exactly for empty slots. `new_slot`: on every device the new slots of the blocks it receives or keeps are distinct and fill 0 up to its new count minus one, at most 8 blocks; some device ends with all 8 slots full. -1 exactly for empty slots.
All inputs are finite; a program needn't handle non-finite values.
Results may differ from the reference program's by a relative error of at most 0.0003.
Values sent between devices are 32-bit elements; how exact they have to be, the bound alone decides.
A program may use at most 256 MiB of HBM per device.

```python
import jax
import jax.numpy as jnp
from jax import lax

BLK = 64
B_DEV = 8
LINKS = 2
MIG = 1
FACE = 4096
SLOTS = 1024


def layout(key):
    device_count = SLOTS // B_DEV
    key_list = jax.random.split(key, 8)
    high_floor = LINKS + 2 * MIG
    high_draw = jax.random.randint(key_list[0], (device_count,), high_floor, B_DEV + 1)
    phase = jax.random.randint(key_list[1], (), 0, 2)
    device_order = jnp.arange(device_count, dtype=jnp.int32)
    is_high = (device_order + phase) % 2 == 0
    counts = jnp.where(is_high, high_draw, LINKS).astype(jnp.int32)
    anchor = jax.random.randint(key_list[2], (), 1, device_count - 9)
    pattern = jnp.array([LINKS, B_DEV, LINKS, B_DEV, LINKS, B_DEV, B_DEV, B_DEV], jnp.int32)
    counts = lax.dynamic_update_slice(counts, pattern, (anchor,))
    previous = jnp.concatenate([counts[:1], counts[:-1]])
    following = jnp.concatenate([counts[1:], counts[-1:]])
    to_left = jnp.minimum(MIG, jnp.maximum(counts - previous, 0) // 2)
    to_right = jnp.minimum(MIG, jnp.maximum(counts - following, 0) // 2)
    kept_count = counts - to_left - to_right
    from_left = jnp.concatenate([jnp.zeros((1,), jnp.int32), to_right[:-1]])
    left_base = jnp.concatenate([jnp.zeros((1,), jnp.int32), (from_left + kept_count)[:-1]])
    slot_ids = lax.broadcasted_iota(jnp.int32, (device_count, B_DEV), 1)
    device_ids = lax.broadcasted_iota(jnp.int32, (device_count, B_DEV), 0)
    valid = slot_ids < counts[:, None]
    stay_end = (counts - to_right)[:, None]
    going_left = slot_ids < to_left[:, None]
    staying = slot_ids < stay_end
    owner = jnp.where(going_left, device_ids - 1, jnp.where(staying, device_ids, device_ids + 1))
    new_place = jnp.where(going_left, left_base[:, None] + slot_ids, jnp.where(staying, from_left[:, None] + slot_ids - to_left[:, None], slot_ids - stay_end))
    owner = jnp.where(valid, owner, -1)
    new_place = jnp.where(valid, new_place, -1)
    successor = (device_order + 1) % device_count
    predecessor = (device_order + device_count - 1) % device_count

    def choose_slots(sub_key):
        score = jax.random.randint(sub_key, (device_count, B_DEV), 0, 2 ** 20)
        score = jnp.where(valid, score, 2 ** 20) * B_DEV + slot_ids
        return jnp.argsort(score, axis=1)[:, :LINKS].astype(jnp.int32)
    high_second = choose_slots(key_list[4])
    low_second = choose_slots(key_list[5])
    high_third = choose_slots(key_list[6])
    low_third = choose_slots(key_list[7])
    device_rows = jnp.arange(device_count, dtype=jnp.int32)[:, None] * jnp.ones((1, LINKS), jnp.int32)
    base_ids = device_ids * B_DEV + slot_ids
    high_first = jnp.where(slot_ids + 1 < counts[:, None], base_ids + 1, -1)
    low_first = jnp.where(valid & (slot_ids > 0), base_ids - 1, -1)
    empty_side = jnp.full((device_count, B_DEV), -1, jnp.int32)
    table = jnp.stack([high_first, low_first, empty_side, empty_side, empty_side, empty_side], 2)
    table = table.at[device_rows, high_second, 2].set(successor[device_rows] * B_DEV + low_second[successor])
    table = table.at[device_rows, low_second, 3].set(predecessor[device_rows] * B_DEV + high_second[predecessor])
    table = table.at[device_rows, high_third, 4].set(predecessor[device_rows] * B_DEV + low_third[predecessor])
    table = table.at[device_rows, low_third, 5].set(successor[device_rows] * B_DEV + high_third[successor])
    return (table.reshape(SLOTS, 6), owner.reshape(SLOTS), new_place.reshape(SLOTS))


def draw_neighbour(key, part):
    return layout(key)[0]


def draw_new_owner(key, part):
    return layout(key)[1]


def draw_new_slot(key, part):
    return layout(key)[2]


def block_scale(key, shape, shards, low, largest):
    def one(dim, parts):
        draws = jax.random.uniform(jax.random.fold_in(jax.random.fold_in(key, 6), dim), (parts,), jnp.float32, low / len(shards), largest / len(shards))
        return jnp.repeat(jnp.exp(draws), shape[dim] // parts).reshape((-1,) + (1,) * (len(shape) - dim - 1))

    gain = one(*shards[0])
    for cut in shards[1:]:
        gain = gain * one(*cut)
    return gain


def setup_inputs(seed: int = 0) -> dict:
    arg_keys = jax.random.split(jax.random.key(seed), 5)
    return {
        "concentration": jnp.clip(0.05 + 0.9 * jax.random.uniform(arg_keys[0], (SLOTS, BLK, FACE), jnp.float32) ** block_scale(arg_keys[0], (SLOTS, BLK, FACE), ((0, 128),), -0.2, 0.2), 0.05, 0.95),
        "neighbour": draw_neighbour(jax.random.fold_in(arg_keys[4], 71), 0),
        "new_owner": draw_new_owner(jax.random.fold_in(arg_keys[4], 71), 0),
        "new_slot": draw_new_slot(jax.random.fold_in(arg_keys[4], 71), 0),
    }


grad_kappa = 2.0
time_step = 0.005
well_height = 1.0
bulk_mobility = 0.3
surface_mobility = 16.0


def faces_of(values):
    blocks, row_count, plane_size = values.shape
    cube = values.reshape(blocks, row_count, row_count, row_count)
    stacked = jnp.stack([
        values[:, row_count - 1, :],
        values[:, 0, :],
        cube[:, :, row_count - 1, :].reshape(blocks, plane_size),
        cube[:, :, 0, :].reshape(blocks, plane_size),
        cube[:, :, :, row_count - 1].reshape(blocks, plane_size),
        cube[:, :, :, 0].reshape(blocks, plane_size)], 1)
    return stacked.reshape(blocks * 6, plane_size)


def beside(values, halo_rows):
    blocks, row_count, plane_size = values.shape
    layers = halo_rows.reshape(blocks, 6, plane_size)
    first_high = jnp.concatenate([values[:, 1:, :], layers[:, 0:1, :]], 1)
    first_low = jnp.concatenate([layers[:, 1:2, :], values[:, :-1, :]], 1)
    second_high = jnp.concatenate([values[:, :, row_count:], layers[:, 2, :].reshape(blocks, row_count, row_count)], 2)
    second_low = jnp.concatenate([layers[:, 3, :].reshape(blocks, row_count, row_count), values[:, :, :-row_count]], 2)
    column = lax.broadcasted_iota(jnp.int32, (1, 1, plane_size), 2) % row_count
    shape_four = (blocks, row_count, row_count, row_count)
    upper_layer = jnp.broadcast_to(layers[:, 4, :].reshape(blocks, row_count, row_count, 1), shape_four).reshape(blocks, row_count, plane_size)
    lower_layer = jnp.broadcast_to(layers[:, 5, :].reshape(blocks, row_count, row_count, 1), shape_four).reshape(blocks, row_count, plane_size)
    third_high = jnp.where(column == row_count - 1, upper_layer, jnp.concatenate([values[:, :, 1:], values[:, :, :1]], 2))
    third_low = jnp.where(column == 0, lower_layer, jnp.concatenate([values[:, :, -1:], values[:, :, :-1]], 2))
    return (first_high, first_low, second_high, second_low, third_high, third_low)


def mobility(values):
    return bulk_mobility + surface_mobility * (values * values) * ((1.0 - values) * (1.0 - values))


def potential(values, near_values):
    laplace = near_values[0] + near_values[1] + near_values[2] + near_values[3] + near_values[4] + near_values[5] - 6.0 * values
    return 2.0 * well_height * values * (1.0 - values) * (1.0 - 2.0 * values) - grad_kappa * laplace


def advance(values, near_values, chemical, near_chemical):
    own_mobility = mobility(values)
    flux_total = jnp.zeros_like(values)
    for side_values, side_chemical in zip(near_values, near_chemical):
        flux_total = flux_total + 0.5 * (own_mobility + mobility(side_values)) * (side_chemical - chemical)
    return values + time_step * flux_total


def halo_rows_of(faces, partner, first_block):
    face_count = partner.shape[0] * 6
    positions = jnp.arange(face_count, dtype=jnp.int32)
    target = partner.reshape(face_count)
    facing = jnp.bitwise_xor(positions % 6, 1)
    face_index = jnp.where(target >= 0, target * 6 + facing, first_block * 6 + positions)
    return faces[face_index]


def reference(concentration, neighbour, new_owner, new_slot):
    groups = SLOTS // B_DEV
    field_faces = faces_of(concentration)
    grouped = concentration.reshape(groups, B_DEV, BLK, FACE)
    grouped_links = neighbour.reshape(groups, B_DEV, 6)
    firsts = jnp.arange(groups, dtype=jnp.int32) * B_DEV

    def first_pass(pieces):
        values, partner, first_block = pieces
        return potential(values, beside(values, halo_rows_of(field_faces, partner, first_block)))

    chemical = lax.map(first_pass, (grouped, grouped_links, firsts))
    chemical_faces = faces_of(chemical.reshape(SLOTS, BLK, FACE))

    def second_pass(pieces):
        values, chem_values, partner, first_block = pieces
        near_values = beside(values, halo_rows_of(field_faces, partner, first_block))
        near_chem = beside(chem_values, halo_rows_of(chemical_faces, partner, first_block))
        return advance(values, near_values, chem_values, near_chem)

    stepped = lax.map(second_pass, (grouped, chemical, grouped_links, firsts)).reshape(SLOTS, BLK, FACE)
    destination = jnp.where(new_owner >= 0, new_owner * B_DEV + new_slot, SLOTS)
    source = jnp.full((SLOTS + 1,), -1, jnp.int32).at[destination].set(jnp.arange(SLOTS, dtype=jnp.int32))[:SLOTS]
    return jnp.where((source >= 0)[:, None, None], stepped[jnp.maximum(source, 0)], 0.0)
```

```python
import functools

import jax
import jax.numpy as jnp
from jax import lax
from jax.experimental import pallas as pl
from jax.experimental.pallas import tpu as pltpu
from jax.sharding import PartitionSpec as P

MESH = pl.DeviceIdType.MESH
AXES = ("gx", "gy")
BLOCKS = 8
LANES = 128
PAIRS = 32
SLABS = 8
TOP = 8
ROWS = 80
F32 = jnp.float32


def lanes_of():
    lane = lax.broadcasted_iota(jnp.int32, (8, LANES), 1)
    cell = lane & 63
    return {
        "upper": lane >= 64,
        "odd": (lane & 1) == 1,
        "pair": cell >> 1,
        "last": cell == 63,
        "edge": (cell == 63) | (cell == 0),
    }


def turned(tile, shift):
    shift %= LANES
    return tile if shift == 0 else pltpu.roll(tile, shift, tile.ndim - 1)


def mobility(values):
    square = values - values * values
    return 0.00075 + 0.04 * (square * square)


def slab(xo):
    return pl.ds(pl.multiple_of(TOP + 8 * xo, 8), 8)


def eight(xo):
    return pl.ds(pl.multiple_of(8 * xo, 8), 8)


def first_row(masks, field, scaled, rows):
    z_face = jnp.zeros((8, LANES), F32)
    ends = []
    for yp in range(PAIRS):
        tile = field[yp, rows, :]
        z_face = jnp.where(masks["pair"] == yp, turned(tile, 2 * yp - 63), z_face)
        scaled[yp, rows, :] = mobility(tile)
        if yp in (0, PAIRS - 1):
            ends.append(tile)
    return z_face, jnp.where(masks["upper"], ends[1], ends[0])


def chemical_row(masks, field, chem, rows, base, y_halo, z_halo):
    above, below = pl.ds(base + 1, 8), pl.ds(base - 1, 8)
    z_face = jnp.zeros((8, LANES), F32)
    ends = []
    before = y_halo
    tile = field[0, rows, :]
    swapped = turned(tile, 64)
    for yp in range(PAIRS):
        if yp < PAIRS - 1:
            following = field[yp + 1, rows, :]
            after = turned(following, 64)
        else:
            following, after = None, y_halo
        total = field[yp, above, :] + field[yp, below, :]
        total = total + (swapped + jnp.where(masks["upper"], after, before))
        side = turned(z_halo, 63 - 2 * yp)
        high = jnp.where(masks["last"], side, turned(tile, -1))
        low = jnp.where(masks["edge"] & ~masks["last"], side, turned(tile, 1))
        total = total + (high + low)
        value = tile * (14.0 + tile * (4.0 * tile - 6.0)) - (total + total)
        chem[yp, rows, :] = value
        z_face = jnp.where(masks["pair"] == yp, turned(value, 2 * yp - 63), z_face)
        if yp in (0, PAIRS - 1):
            ends.append(value)
        before, tile, swapped = swapped, following, after
    return z_face, jnp.where(masks["upper"], ends[1], ends[0])


def advance_row(masks, field, chem, scaled, out, rows, out_rows, base, layers, faces):
    field_y, field_z, chem_y, chem_z = layers
    field_face, chem_face = faces
    above, below = pl.ds(base + 1, 8), pl.ds(base - 1, 8)
    side_flux = (mobility(field_face) + mobility(field_z)) * (chem_z - chem_face)
    u_before, m_before = chem_y, mobility(field_y)
    u_halo, m_halo = u_before, m_before
    u, m = chem[0, rows, :], scaled[0, rows, :]
    u_swapped, m_swapped = turned(u, 64), turned(m, 64)
    for yp in range(PAIRS):
        if yp < PAIRS - 1:
            u_next, m_next = chem[yp + 1, rows, :], scaled[yp + 1, rows, :]
            u_after, m_after = turned(u_next, 64), turned(m_next, 64)
        else:
            u_next = m_next = None
            u_after, m_after = u_halo, m_halo
        flux = (m + scaled[yp, above, :]) * (chem[yp, above, :] - u)
        flux = flux + (m + scaled[yp, below, :]) * (chem[yp, below, :] - u)
        flux = flux + (m + m_swapped) * (u_swapped - u)
        u_far = jnp.where(masks["upper"], u_after, u_before)
        m_far = jnp.where(masks["upper"], m_after, m_before)
        flux = flux + (m + m_far) * (u_far - u)
        along = (m + turned(m, -1)) * (turned(u, -1) - u)
        along = jnp.where(masks["last"], 0.0, along)
        outer = jnp.where(masks["edge"], turned(side_flux, 63 - 2 * yp), 0.0)
        flux = flux + (along - turned(along, 1) + outer)
        out[yp, out_rows, :] = field[yp, rows, :] + flux
        u_before, m_before = u_swapped, m_swapped
        u, m, u_swapped, m_swapped = u_next, m_next, u_after, m_after


def place():
    size = lax.axis_size(AXES)
    minor = lax.axis_size("gy")
    me = lax.axis_index("gx") * minor + lax.axis_index("gy")
    upper, lower = lax.rem(me + 1, size), lax.rem(me + size - 1, size)

    def coordinates(device):
        return (device // minor, lax.rem(device, minor))

    return me, coordinates(upper), coordinates(lower)


def remote(source, target, send, receive, device):
    return pltpu.make_async_remote_copy(
        source, target, send, receive, device_id=device, device_id_type=MESH
    )


def own_kernel(
    c_hbm, links, owner, slot, field, got, got_layers, got_marks,
    scaled, chem, right, y_c, z_c, y_u, z_u, sent_c, sent_u, came_c, came_u, packed, marks, table,
    load_sem, face_send, face_recv, block_send, block_recv, pack_send, pack_recv,
):
    me, upper, lower = place()
    masks = lanes_of()
    full = {
        "upper": lax.broadcasted_iota(jnp.int32, (64, LANES), 1) >= 64,
        "odd": (lax.broadcasted_iota(jnp.int32, (64, LANES), 1) & 1) == 1,
    }

    def load(b, xo):
        return pltpu.make_async_copy(c_hbm.at[b, xo], field.at[b, :, slab(xo), :], load_sem.at[b, xo])

    @pl.loop(0, BLOCKS * SLABS)
    def _(i):
        load(i // SLABS, i % SLABS).start()

    barrier = pltpu.get_barrier_semaphore()
    for device in (upper, lower):
        pl.semaphore_signal(barrier, inc=1, device_id=device, device_id_type=MESH)

    def link(b, d):
        return links[b * 6 + d]

    def scan(d):
        least, first, second = jnp.int32(BLOCKS), jnp.int32(BLOCKS - 1), jnp.int32(0)
        for b in range(BLOCKS):
            p = link(b, d)
            far = (p >= 0) & ((p >> 3) != me)
            least = jnp.where(far, jnp.minimum(least, p & 7), least)
            first = jnp.where(far, jnp.minimum(first, b), first)
            second = jnp.where(far, b, second)
        return least, first, second

    near_base = {2: 8, 3: 8, 4: 8, 5: 16}
    far_base = {2: 18, 3: 16, 4: 24, 5: 26}
    picks = {}
    for d in (2, 3, 4, 5):
        least, first, second = scan(d)
        picks[d] = (first, second)
        for b in range(BLOCKS):
            p = link(b, d)
            part = p & 7
            far = far_base[d] + (part > least).astype(jnp.int32)
            near = jnp.where((p >> 3) == me, near_base[d] + part, far)
            table[b * 6 + d] = jnp.where(p < 0, b, near)
    moving, mark_right, mark_left = jnp.int32(0), jnp.int32(0), jnp.int32(0)
    for b in range(BLOCKS):
        goes_right, goes_left = owner[b] == me + 1, owner[b] == me - 1
        moving = jnp.where(goes_right, b, moving)
        mark_right = jnp.where(goes_right, slot[b] + 1, mark_right)
        mark_left = jnp.where((owner[b] >= 0) & goes_left, slot[b] + 1, mark_left)
    marks[0] = jnp.full((8, LANES), mark_right, jnp.int32).astype(F32)
    marks[1] = jnp.full((8, LANES), mark_left, jnp.int32).astype(F32)

    def keep_faces(y_table, z_table, b, xo, y_face, z_face):
        part = eight(xo)
        y_table[b, part, :] = y_face
        y_table[BLOCKS + b, part, :] = turned(y_face, 64)
        z_table[b, part, :] = z_face
        z_table[BLOCKS + b, part, :] = turned(z_face, 63)
        z_table[2 * BLOCKS + b, part, :] = turned(z_face, 65)

    @pl.loop(0, BLOCKS * SLABS)
    def _(i):
        load(i // SLABS, i % SLABS).wait()

    @pl.loop(0, BLOCKS * SLABS)
    def _(i):
        b, xo = i // SLABS, i % SLABS
        z_face, y_face = first_row(masks, field.at[b], scaled.at[b], slab(xo))
        keep_faces(y_c, z_c, b, xo, y_face, z_face)

    pl.semaphore_wait(barrier, 2)

    def fill(message, y_table, z_table):
        message[0, 0] = jnp.where(
            full["upper"], y_table[picks[2][0]], turned(y_table[picks[2][1]], 64)
        )
        message[0, 1] = jnp.where(
            full["odd"], z_table[picks[5][0]], turned(z_table[picks[5][1]], -1)
        )
        message[1, 0] = jnp.where(
            full["upper"], turned(y_table[picks[3][1]], 64), y_table[picks[3][0]]
        )
        message[1, 1] = jnp.where(
            full["odd"], turned(z_table[picks[4][1]], 1), z_table[picks[4][0]]
        )

    def face_copies(k, message, came):
        return [
            remote(message.at[side], came.at[side], face_send.at[k, side], face_recv.at[k, side], device)
            for side, device in enumerate((upper, lower))
        ]

    def take(came, y_table, z_table):
        low_y, low_z, high_y, high_z = came[0, 0], came[0, 1], came[1, 0], came[1, 1]
        y_table[16], y_table[17] = turned(low_y, 64), low_y
        y_table[18], y_table[19] = turned(high_y, 64), high_y
        z_table[24], z_table[25] = turned(low_z, 63), turned(low_z, 64)
        z_table[26], z_table[27] = turned(high_z, 65), turned(high_z, 64)

    def outside(y_table, z_table, b, part):
        y_layer = jnp.where(
            masks["upper"] if part is not None else full["upper"],
            *(
                y_table[table[b * 6 + d], part, :] if part is not None else y_table[table[b * 6 + d]]
                for d in (2, 3)
            ),
        )
        z_up, z_down = (
            z_table[table[b * 6 + d], part, :] if part is not None else z_table[table[b * 6 + d]]
            for d in (4, 5)
        )
        return y_layer, jnp.where(masks["odd"] if part is not None else full["odd"], z_down, z_up)

    def x_layers(values, b):
        high, low = link(b, 0), link(b, 1)
        high_block = jnp.where(high < 0, b, high & 7)
        low_block = jnp.where(low < 0, b, low & 7)
        from_low = jnp.where(low < 0, values[b, :, 8:9, :], values[low_block, :, 71:72, :])
        from_high = jnp.where(high < 0, values[b, :, 71:72, :], values[high_block, :, 8:9, :])
        return from_low, from_high

    fill(sent_c, y_c, z_c)
    first_faces = face_copies(0, sent_c, came_c)
    for copy in first_faces:
        copy.start()

    @pl.loop(0, SLABS)
    def _(xo):
        for yp in range(PAIRS):
            right[xo, yp] = field[moving, yp, slab(xo), :]

    def block_copies(xo):
        target = slab(xo)
        return [
            remote(right.at[xo], got.at[0, :, target, :], block_send.at[0, xo], block_recv.at[0, xo], upper),
            remote(c_hbm.at[0, xo], got.at[1, :, target, :], block_send.at[1, xo], block_recv.at[1, xo], lower),
        ]

    early = 3
    for xo in range(early):
        for copy in block_copies(xo):
            copy.start()

    @pl.loop(0, BLOCKS)
    def _(b):
        from_low, from_high = x_layers(field, b)
        field[b, :, 7:8, :] = from_low
        field[b, :, 72:73, :] = from_high
        scaled[b, :, 7:8, :] = mobility(from_low)
        scaled[b, :, 72:73, :] = mobility(from_high)

    for copy in first_faces:
        copy.wait_recv()
    take(came_c, y_c, z_c)

    @pl.loop(0, BLOCKS * SLABS)
    def _(i):
        b, xo = i // SLABS, i % SLABS
        y_halo, z_halo = outside(y_c, z_c, b, eight(xo))
        z_face, y_face = chemical_row(
            masks, field.at[b], chem.at[b], slab(xo), TOP + 8 * xo, y_halo, z_halo
        )
        keep_faces(y_u, z_u, b, xo, y_face, z_face)

    fill(sent_u, y_u, z_u)
    second_faces = face_copies(1, sent_u, came_u)
    for copy in second_faces:
        copy.start()
    for xo in range(early, SLABS):
        for copy in block_copies(xo):
            copy.start()

    @pl.loop(0, BLOCKS)
    def _(b):
        from_low, from_high = x_layers(chem, b)
        chem[b, :, 7:8, :] = from_low
        chem[b, :, 72:73, :] = from_high

    def pack(k, values, y_table, z_table):
        for side, b in ((0, moving), (1, 0)):
            y_layer, z_layer = outside(y_table, z_table, b, None)
            packed[side, k, 0] = y_layer
            packed[side, k, 1] = z_layer
            for yp in range(PAIRS):
                packed[side, k, 2, yp : yp + 1, :] = values[b, yp, 7:8, :]
                packed[side, k, 2, PAIRS + yp : PAIRS + yp + 1, :] = values[b, yp, 72:73, :]

    pack(0, field, y_c, z_c)
    for copy in second_faces:
        copy.wait_recv()
    take(came_u, y_u, z_u)
    pack(1, chem, y_u, z_u)
    pack_copies = []
    for side, device in enumerate((upper, lower)):
        pack_copies.append(
            remote(packed.at[side], got_layers.at[side], pack_send.at[0, side], pack_recv.at[0, side], device)
        )
        pack_copies.append(
            remote(marks.at[side], got_marks.at[side], pack_send.at[1, side], pack_recv.at[1, side], device)
        )
    for copy in pack_copies:
        copy.start()

    @pl.loop(0, BLOCKS * SLABS)
    def _(i):
        b, xo = i // SLABS, i % SLABS
        part = eight(xo)
        layers = outside(y_c, z_c, b, part) + outside(y_u, z_u, b, part)
        faces = (z_c[b, part, :], z_u[b, part, :])
        rows = slab(xo)
        advance_row(
            masks, field.at[b], chem.at[b], scaled.at[b], field.at[b], rows, rows, TOP + 8 * xo, layers, faces
        )

    for copy in pack_copies:
        copy.wait()
    for xo in range(SLABS):
        for copy in block_copies(xo):
            copy.wait()
    for copy in first_faces + second_faces:
        copy.wait_send()


def layout_kernel(
    field, got, got_layers, got_marks, owner, slot, out,
    arrived, scaled, chem, stepped, zeros, z_c, z_u, keep_sem, zero_sem, new_sem,
):
    me, _, _ = place()
    masks = lanes_of()
    kept = jnp.int32(0)
    for b in range(BLOCKS):
        stays = owner[b] == me
        kept = kept + stays.astype(jnp.int32)

        @pl.when(stays)
        def _(b=b):
            for xo in range(SLABS):
                pltpu.make_async_copy(
                    field.at[b, :, pl.ds(TOP + 8 * xo, 8), :], out.at[slot[b], xo], keep_sem.at[b, xo]
                ).start()

    places = [jnp.max(got_marks[side]).astype(jnp.int32) for side in range(2)]
    count = kept
    for target in places:
        count = count + (target > 0).astype(jnp.int32)
    zeros[...] = jnp.zeros_like(zeros)
    for s in range(BLOCKS):

        @pl.when(s >= count)
        def _(s=s):
            pltpu.make_async_copy(zeros, out.at[s], zero_sem.at[s]).start()

    for side in range(2):

        @pl.when(places[side] > 0)
        def _(side=side):
            layers = got_layers.at[side]

            @pl.loop(0, SLABS)
            def _(xo):
                rows = slab(xo)
                for yp in range(PAIRS):
                    arrived[yp, rows, :] = got[side, yp, rows, :]
                z_face, _ = first_row(masks, arrived, scaled, rows)
                z_c[eight(xo), :] = z_face

            for yp in range(PAIRS):
                for k, values in ((0, arrived), (1, chem)):
                    values[yp, 7:8, :] = layers[k, 2, yp : yp + 1, :]
                    values[yp, 72:73, :] = layers[k, 2, PAIRS + yp : PAIRS + yp + 1, :]
                scaled[yp, 7:8, :] = mobility(layers[0, 2, yp : yp + 1, :])
                scaled[yp, 72:73, :] = mobility(layers[0, 2, PAIRS + yp : PAIRS + yp + 1, :])

            @pl.loop(0, SLABS)
            def _(xo):
                part = eight(xo)
                z_face, _ = chemical_row(
                    masks, arrived, chem, slab(xo), TOP + 8 * xo, layers[0, 0, part, :], layers[0, 1, part, :]
                )
                z_u[part, :] = z_face

            @pl.loop(0, SLABS)
            def _(xo):
                part = eight(xo)
                around = (layers[0, 0, part, :], layers[0, 1, part, :], layers[1, 0, part, :], layers[1, 1, part, :])
                advance_row(
                    masks, arrived, chem, scaled, stepped.at[side, xo], slab(xo), pl.ds(0, 8), TOP + 8 * xo,
                    around, (z_c[part, :], z_u[part, :]),
                )

            pltpu.make_async_copy(stepped.at[side], out.at[places[side] - 1], new_sem.at[side]).start()

    for b in range(BLOCKS):

        @pl.when(owner[b] == me)
        def _(b=b):
            for xo in range(SLABS):
                pltpu.make_async_copy(
                    field.at[b, :, pl.ds(TOP + 8 * xo, 8), :], out.at[slot[b], xo], keep_sem.at[b, xo]
                ).wait()

    for s in range(BLOCKS):

        @pl.when(s >= count)
        def _(s=s):
            pltpu.make_async_copy(zeros, out.at[s], zero_sem.at[s]).wait()

    for side in range(2):

        @pl.when(places[side] > 0)
        def _(side=side):
            pltpu.make_async_copy(stepped.at[side], out.at[places[side] - 1], new_sem.at[side]).wait()


def per_device(concentration, neighbour, new_owner, new_slot):
    tiles = concentration.reshape(BLOCKS, SLABS, 8, PAIRS, LANES).transpose(0, 1, 3, 2, 4)
    links = neighbour.reshape(BLOCKS * 6)
    anywhere = pl.BlockSpec(memory_space=pl.ANY)
    scalars = pl.BlockSpec(memory_space=pltpu.SMEM)
    vector = pl.BlockSpec(memory_space=pltpu.VMEM)
    padded = (PAIRS, ROWS, LANES)
    face = (64, LANES)
    tables = [pltpu.VMEM((20, *face), F32), pltpu.VMEM((28, *face), F32)]
    dma = pltpu.SemaphoreType.DMA
    field, got, got_layers, got_marks = pl.pallas_call(
        own_kernel,
        out_shape=[
            pltpu.VMEM((BLOCKS, *padded), F32),
            pltpu.VMEM((2, *padded), F32),
            pltpu.VMEM((2, 2, 3, *face), F32),
            pltpu.VMEM((2, 8, LANES), F32),
        ],
        in_specs=[anywhere, scalars, scalars, scalars],
        out_specs=[vector] * 4,
        scratch_shapes=[
            pltpu.VMEM((BLOCKS, *padded), F32),
            pltpu.VMEM((BLOCKS, *padded), F32),
            pltpu.VMEM((SLABS, PAIRS, 8, LANES), F32),
            *tables,
            *tables,
            *[pltpu.VMEM((2, 2, *face), F32)] * 4,
            pltpu.VMEM((2, 2, 3, *face), F32),
            pltpu.VMEM((2, 8, LANES), F32),
            pltpu.SMEM((BLOCKS * 6,), jnp.int32),
            dma((BLOCKS, SLABS)),
            dma((2, 2)),
            dma((2, 2)),
            dma((2, SLABS)),
            dma((2, SLABS)),
            dma((2, 2)),
            dma((2, 2)),
        ],
        compiler_params=pltpu.CompilerParams(
            collective_id=0, has_side_effects=True, vmem_limit_bytes=48 << 20
        ),
    )(tiles, links, new_owner, new_slot)
    out = pl.pallas_call(
        layout_kernel,
        out_shape=jax.ShapeDtypeStruct((BLOCKS, SLABS, PAIRS, 8, LANES), F32),
        in_specs=[vector] * 4 + [scalars] * 2,
        out_specs=anywhere,
        scratch_shapes=[
            pltpu.VMEM(padded, F32),
            pltpu.VMEM(padded, F32),
            pltpu.VMEM(padded, F32),
            pltpu.VMEM((2, SLABS, PAIRS, 8, LANES), F32),
            pltpu.VMEM((SLABS, PAIRS, 8, LANES), F32),
            pltpu.VMEM(face, F32),
            pltpu.VMEM(face, F32),
            dma((BLOCKS, SLABS)),
            dma((BLOCKS,)),
            dma((2,)),
        ],
        compiler_params=pltpu.CompilerParams(vmem_limit_bytes=40 << 20),
    )(field, got, got_layers, got_marks, new_owner, new_slot)
    return out.transpose(0, 1, 3, 2, 4).reshape(concentration.shape)


def solution(mesh):
    return jax.shard_map(
        per_device,
        mesh=mesh,
        in_specs=(P(AXES, None, None), P(AXES, None), P(AXES), P(AXES)),
        out_specs=P(AXES, None, None),
        check_vma=False,
    )
```

```python
import jax
import jax.numpy as jnp
from jax import lax
from jax.experimental import pallas as pl
from jax.experimental.pallas import tpu as pltpu
from jax.sharding import PartitionSpec as P

MESH = pl.DeviceIdType.MESH
AXES = ("gx", "gy")
BLOCKS = 8
LANES = 128
TILES = 32
SLABS = 8
TOP = 8
PITCH = 80
F32 = jnp.float32
FACE = (32, LANES)


def masks_of():
    lane = lax.broadcasted_iota(jnp.int32, (8, LANES), 1)
    xc, yc = lane & 15, lane >> 4
    return {
        "xc": xc,
        "yc": yc,
        "x_first": xc == 0,
        "x_last": xc == 15,
        "y_first": yc == 0,
        "y_last": yc == 7,
    }


def turned(tile, shift):
    if isinstance(shift, int):
        shift %= LANES
        if shift == 0:
            return tile
    return pltpu.roll(tile, shift, 1)


def mobility(values):
    square = values - values * values
    return 0.00075 + 0.04 * (square * square)


def slab(z, offset=0):
    if offset:
        return pl.ds(TOP + 8 * z + offset, 8)
    return pl.ds(pl.multiple_of(TOP + 8 * z, 8), 8)


def eight(z):
    return pl.ds(pl.multiple_of(8 * z, 8), 8)


def part(k):
    return pl.ds(8 * k, 8)


def rows_of(block):
    return block.reshape(TILES * PITCH, LANES)


def z_rows(block, row):
    return rows_of(block)[pl.ds(row, TILES, stride=PITCH), :]


def set_z_rows(block, row, values):
    rows_of(block)[pl.ds(row, TILES, stride=PITCH), :] = values


def shifted_sides(masks, block, z, halo):
    rows = slab(z)
    sides = []
    for yf in range(8):
        own = turned(block[yf, rows, :], -1)
        sides.append(jnp.where(masks["x_last"], halo(0, yf), own))
    for yf in range(8):
        own = turned(block[24 + yf, rows, :], 1)
        sides.append(jnp.where(masks["x_first"], halo(1, yf), own))
    for xf in range(4):
        own = turned(block[8 * xf, rows, :], -16)
        sides.append(jnp.where(masks["y_last"], halo(2, xf), own))
    for xf in range(4):
        own = turned(block[8 * xf + 7, rows, :], 16)
        sides.append(jnp.where(masks["y_first"], halo(3, xf), own))
    return sides


def near(block, z, sides, xf, yf):
    rows, tile = slab(z), 8 * xf + yf
    return (
        block[tile + 8, rows, :] if xf < 3 else sides[yf],
        block[tile - 8, rows, :] if xf > 0 else sides[8 + yf],
        block[tile + 1, rows, :] if yf < 7 else sides[16 + xf],
        block[tile - 1, rows, :] if yf > 0 else sides[20 + xf],
        block[tile, slab(z, 1), :],
        block[tile, slab(z, -1), :],
    )


def chemical_slab(masks, field, chem, side_mobility, z, halo, keep):
    sides = shifted_sides(masks, field, z, halo)
    for k, values in enumerate(sides):
        side_mobility[k, eight(z), :] = mobility(values)
    rows = slab(z)
    for xf in range(4):
        for yf in range(8):
            tile = field[8 * xf + yf, rows, :]
            a, b, c, d, e, f = near(field, z, sides, xf, yf)
            total = ((a + b) + (c + d)) + (e + f)
            value = tile * (14.0 + tile * (4.0 * tile - 6.0)) - (total + total)
            chem[8 * xf + yf, rows, :] = value
            if keep is not None and yf in (0, 7):
                keep(xf, yf, value)


def advance_slab(masks, field, chem, scaled, side_mobility, out, z, halo):
    sides = shifted_sides(masks, chem, z, halo)
    side_scaled = [side_mobility[k, eight(z), :] for k in range(24)]
    rows = slab(z)
    for xf in range(4):
        for yf in range(8):
            tile = 8 * xf + yf
            u, m = chem[tile, rows, :], scaled[tile, rows, :]
            flux = None
            for u_near, m_near in zip(near(chem, z, sides, xf, yf), near(scaled, z, side_scaled, xf, yf)):
                term = (m + m_near) * (u_near - u)
                flux = term if flux is None else flux + term
            out[tile, rows, :] = field[tile, rows, :] + flux


def y_part(masks, tile, yf, z, held):
    shift = lax.rem((z - (7 if yf else 0)) * 16 + LANES, LANES)
    return jnp.where(masks["yc"] == z, turned(tile, shift), held)


def y_halo(face, side, xf, z):
    place = 7 if side == 2 else 0
    return turned(face[part(xf), :], lax.rem((place - z) * 16 + LANES, LANES))


def x_halo(face, side, yf, z):
    place = 15 if side == 0 else 0
    spot = (yf & 1) * 8 + z
    return turned(face[part(yf >> 1), :], lax.rem(place - spot + LANES, LANES))


def group_in(stage, xf, pair):
    rows = [stage[4 * yc + pair, pl.ds(xf, 16, stride=4), :] for yc in range(8)]
    return jnp.concatenate(rows, 0).T


def group_out(stage, xf, pair, block):
    tile = 8 * xf + 2 * pair
    both = jnp.concatenate([block[tile, TOP : TOP + 64, :], block[tile + 1, TOP : TOP + 64, :]], 0).T
    for yc in range(8):
        stage[4 * yc + pair, pl.ds(xf, 16, stride=4), :] = both[16 * yc : 16 * yc + 16]


def place():
    size = lax.axis_size(AXES)
    minor = lax.axis_size("gy")
    me = lax.axis_index("gx") * minor + lax.axis_index("gy")
    upper, lower = lax.rem(me + 1, size), lax.rem(me + size - 1, size)

    def coordinates(device):
        return (device // minor, lax.rem(device, minor))

    return me, coordinates(upper), coordinates(lower)


def remote(source, target, send, receive, device):
    return pltpu.make_async_remote_copy(
        source, target, send, receive, device_id=device, device_id_type=MESH
    )


def own_kernel(
    c_hbm, links, owner, slot, stage, got, got_layers, got_marks,
    field, chem, scaled, side_mobility, pay, y_c, z_c, y_u, z_u, sent_c, sent_u, came_c, came_u, packed, marks, table,
    load_sem, face_send, face_recv, block_send, block_recv, pack_send, pack_recv,
):
    me, upper, lower = place()
    masks = masks_of()

    def load(b, xo):
        return pltpu.make_async_copy(c_hbm.at[b, xo], stage.at[b, :, eight(xo), :], load_sem.at[b, xo])

    @pl.loop(0, BLOCKS * SLABS)
    def _(i):
        load(i // SLABS, i % SLABS).start()

    barrier = pltpu.get_barrier_semaphore()
    for device in (upper, lower):
        pl.semaphore_signal(barrier, inc=1, device_id=device, device_id_type=MESH)

    def link(b, d):
        return links[b * 6 + d]

    near_base = {2: 0, 3: 8, 4: 0, 5: 8}
    far_base = {2: 18, 3: 16, 4: 16, 5: 18}
    own_base = {2: 8, 3: 0, 4: 8, 5: 0}
    picks = {}
    for d in (2, 3, 4, 5):
        least, first, second = jnp.int32(BLOCKS), jnp.int32(BLOCKS - 1), jnp.int32(0)
        for b in range(BLOCKS):
            p = link(b, d)
            far = (p >= 0) & ((p >> 3) != me)
            least = jnp.where(far, jnp.minimum(least, p & 7), least)
            first = jnp.where(far, jnp.minimum(first, b), first)
            second = jnp.where(far, b, second)
        picks[d] = (first + own_base[d], second + own_base[d])
        for b in range(BLOCKS):
            p = link(b, d)
            far = far_base[d] + ((p & 7) > least).astype(jnp.int32)
            index = jnp.where((p >> 3) == me, near_base[d] + (p & 7), far)
            table[b * 6 + d] = jnp.where(p < 0, own_base[d] + b, index)
    moving, mark_right, mark_left = jnp.int32(0), jnp.int32(0), jnp.int32(0)
    for b in range(BLOCKS):
        goes_right, goes_left = owner[b] == me + 1, owner[b] == me - 1
        moving = jnp.where(goes_right, b, moving)
        mark_right = jnp.where(goes_right, slot[b] + 1, mark_right)
        mark_left = jnp.where((owner[b] >= 0) & goes_left, slot[b] + 1, mark_left)
    marks[0] = jnp.full((8, LANES), mark_right, jnp.int32).astype(F32)
    marks[1] = jnp.full((8, LANES), mark_left, jnp.int32).astype(F32)

    def take_in(b, xf, pair, extra=None):
        both = group_in(stage.at[b], xf, pair)
        for h in range(2):
            tile, values = 8 * xf + 2 * pair + h, both[64 * h : 64 * h + 64]
            if extra is None:
                field[b, tile, TOP : TOP + 64, :] = values
                scaled[b, tile, TOP : TOP + 64, :] = mobility(values)
            else:
                pay[extra, tile] = values

    @pl.loop(0, BLOCKS)
    def _(b):
        for xo in range(SLABS):
            load(b, xo).wait()

        @pl.loop(0, 8)
        def _(k):
            for q in range(2):
                take_in(b, k // 2, (k % 2) * 2 + q)

    @pl.loop(0, 8)
    def _(k):
        for q in range(2):
            take_in(moving, k // 2, (k % 2) * 2 + q, 0)

    @pl.loop(0, TILES)
    def _(t):
        pay[1, t] = field[0, t, TOP : TOP + 64, :]

    def z_faces(values, z_table):
        @pl.loop(0, BLOCKS)
        def _(b):
            z_table[b] = z_rows(values.at[b], TOP)
            z_table[BLOCKS + b] = z_rows(values.at[b], TOP + 63)

    z_faces(field, z_c)

    def keep_y(y_table, b, z):
        def keep(xf, yf, value):
            entry = BLOCKS + b if yf else b
            y_table[entry, part(xf), :] = y_part(masks, value, yf, z, y_table[entry, part(xf), :])

        return keep

    @pl.loop(0, BLOCKS * SLABS)
    def _(i):
        b, z = i // SLABS, i % SLABS
        keep = keep_y(y_c, b, z)
        for xf in range(4):
            for yf in (0, 7):
                keep(xf, yf, field[b, 8 * xf + yf, slab(z), :])

    pl.semaphore_wait(barrier, 2)

    def fill(message, y_table, z_table):
        for side, (y_dir, z_dir) in enumerate(((2, 5), (3, 4))):
            for k in range(2):
                message[side, k] = y_table[picks[y_dir][k]]
                message[side, 2 + k] = z_table[picks[z_dir][k]]

    def face_copies(k, message, came):
        return [
            remote(message.at[side], came.at[side], face_send.at[k, side], face_recv.at[k, side], device)
            for side, device in enumerate((upper, lower))
        ]

    def take(came, y_table, z_table):
        for side in range(2):
            for k in range(2):
                y_table[16 + 2 * side + k] = came[side, k]
                z_table[16 + 2 * side + k] = came[side, 2 + k]

    def block_copies(z):
        return [
            remote(
                pay.at[side, :, eight(z), :], got.at[side, :, slab(z), :],
                block_send.at[side, z], block_recv.at[side, z], device,
            )
            for side, device in enumerate((upper, lower))
        ]

    def halo_of(values, y_table, b, z):
        rows = slab(z)
        open_high, open_low = link(b, 0) < 0, link(b, 1) < 0
        high = jnp.where(open_high, b, link(b, 0) & 7)
        low = jnp.where(open_low, b, link(b, 1) & 7)

        def halo(side, k):
            if side == 0:
                return jnp.where(open_high, values[b, 24 + k, rows, :], turned(values[high, k, rows, :], 15))
            if side == 1:
                return jnp.where(open_low, values[b, k, rows, :], turned(values[low, 24 + k, rows, :], -15))
            return y_halo(y_table.at[table[b * 6 + side]], side, k, z)

        return halo

    def set_z(values, z_table, b, scale=None):
        for row, d in ((TOP + 64, 4), (TOP - 1, 5)):
            layer = z_table[table[b * 6 + d]]
            set_z_rows(values.at[b], row, layer)
            if scale is not None:
                set_z_rows(scale.at[b], row, mobility(layer))

    fill(sent_c, y_c, z_c)
    first_faces = face_copies(0, sent_c, came_c)
    for copy in first_faces:
        copy.start()
    early = 3
    for z in range(early):
        for copy in block_copies(z):
            copy.start()
    for copy in first_faces:
        copy.wait_recv()
    take(came_c, y_c, z_c)

    @pl.loop(0, BLOCKS)
    def _(b):
        set_z(field, z_c, b, scaled)

    @pl.loop(0, BLOCKS * SLABS)
    def _(i):
        b, z = i // SLABS, i % SLABS
        chemical_slab(
            masks, field.at[b], chem.at[b], side_mobility.at[b], z, halo_of(field, y_c, b, z), keep_y(y_u, b, z)
        )

    z_faces(chem, z_u)
    fill(sent_u, y_u, z_u)
    second_faces = face_copies(1, sent_u, came_u)
    for copy in second_faces:
        copy.start()
    for z in range(early, SLABS):
        for copy in block_copies(z):
            copy.start()

    def pack(k, values, y_table, z_table):
        for side, b in ((0, moving), (1, 0)):
            for d in (2, 3):
                packed[side, k, d] = y_table[table[b * 6 + d]]
            for d in (4, 5):
                packed[side, k, d] = z_table[table[b * 6 + d]]

            @pl.loop(0, SLABS)
            def _(z, side=side, b=b):
                halo = halo_of(values, y_table, b, z)
                for d in range(2):
                    for yf in range(8):
                        spot = (yf & 1) * 8 + z
                        shift = lax.rem(spot - (0 if d else 15) + LANES, LANES)
                        held = packed[side, k, d, part(yf >> 1), :]
                        packed[side, k, d, part(yf >> 1), :] = jnp.where(
                            masks["xc"] == spot, turned(halo(d, yf), shift), held
                        )

    pack(0, field, y_c, z_c)
    for copy in second_faces:
        copy.wait_recv()
    take(came_u, y_u, z_u)

    @pl.loop(0, BLOCKS)
    def _(b):
        set_z(chem, z_u, b)

    pack(1, chem, y_u, z_u)
    pack_copies = []
    for side, device in enumerate((upper, lower)):
        pack_copies.append(
            remote(packed.at[side], got_layers.at[side], pack_send.at[0, side], pack_recv.at[0, side], device)
        )
        pack_copies.append(
            remote(marks.at[side], got_marks.at[side], pack_send.at[1, side], pack_recv.at[1, side], device)
        )
    for copy in pack_copies:
        copy.start()

    @pl.loop(0, BLOCKS * SLABS)
    def _(i):
        b, z = i // SLABS, i % SLABS
        advance_slab(
            masks, field.at[b], chem.at[b], scaled.at[b], side_mobility.at[b], field.at[b], z,
            halo_of(chem, y_u, b, z),
        )

    @pl.loop(0, BLOCKS * 8)
    def _(i):
        b, k = i // 8, i % 8
        for q in range(2):
            group_out(stage.at[b], k // 2, (k % 2) * 2 + q, field.at[b])

    for copy in pack_copies:
        copy.wait()
    for z in range(SLABS):
        for copy in block_copies(z):
            copy.wait()
    for copy in first_faces + second_faces:
        copy.wait_send()


def layout_kernel(
    stage, got, got_layers, got_marks, owner, slot, out,
    arrived, scaled, chem, stepped, side_mobility, final, zeros, keep_sem, zero_sem, new_sem,
):
    me, _, _ = place()
    masks = masks_of()

    def keep_copy(b, xo):
        return pltpu.make_async_copy(stage.at[b, :, 8 * xo : 8 * xo + 8, :], out.at[slot[b], xo], keep_sem.at[b, xo])

    def new_copy(side, xo):
        return pltpu.make_async_copy(
            final.at[side, :, 8 * xo : 8 * xo + 8, :], out.at[places[side] - 1, xo], new_sem.at[side, xo]
        )

    kept = jnp.int32(0)
    for b in range(BLOCKS):
        stays = owner[b] == me
        kept = kept + stays.astype(jnp.int32)

        @pl.when(stays)
        def _(b=b):
            for xo in range(SLABS):
                keep_copy(b, xo).start()

    places = [jnp.max(got_marks[side]).astype(jnp.int32) for side in range(2)]
    count = kept
    for target in places:
        count = count + (target > 0).astype(jnp.int32)
    zeros[...] = jnp.zeros_like(zeros)
    for s in range(BLOCKS):

        @pl.when(s >= count)
        def _(s=s):
            pltpu.make_async_copy(zeros, out.at[s], zero_sem.at[s]).start()

    for side in range(2):

        @pl.when(places[side] > 0)
        def _(side=side):
            layers = got_layers.at[side]

            def halo_of(k, z):
                def halo(d, f):
                    return (x_halo if d < 2 else y_halo)(layers.at[k, d], d, f, z)

                return halo

            @pl.loop(0, SLABS)
            def _(z):
                rows = slab(z)
                for t in range(TILES):
                    values = got[side, t, rows, :]
                    arrived[t, rows, :] = values
                    scaled[t, rows, :] = mobility(values)

            for row, d in ((TOP + 64, 4), (TOP - 1, 5)):
                set_z_rows(arrived, row, layers[0, d])
                set_z_rows(scaled, row, mobility(layers[0, d]))
                set_z_rows(chem, row, layers[1, d])

            @pl.loop(0, SLABS)
            def _(z):
                chemical_slab(masks, arrived, chem, side_mobility, z, halo_of(0, z), None)

            @pl.loop(0, SLABS)
            def _(z):
                advance_slab(masks, arrived, chem, scaled, side_mobility, stepped, z, halo_of(1, z))

            @pl.loop(0, 8)
            def _(k):
                for q in range(2):
                    group_out(final.at[side], k // 2, (k % 2) * 2 + q, stepped)

            for xo in range(SLABS):
                new_copy(side, xo).start()

    for b in range(BLOCKS):

        @pl.when(owner[b] == me)
        def _(b=b):
            for xo in range(SLABS):
                keep_copy(b, xo).wait()

    for s in range(BLOCKS):

        @pl.when(s >= count)
        def _(s=s):
            pltpu.make_async_copy(zeros, out.at[s], zero_sem.at[s]).wait()

    for side in range(2):

        @pl.when(places[side] > 0)
        def _(side=side):
            for xo in range(SLABS):
                new_copy(side, xo).wait()


def per_device(concentration, neighbour, new_owner, new_slot):
    tiles = concentration.reshape(BLOCKS, SLABS, 8, 32, LANES).transpose(0, 1, 3, 2, 4)
    links = neighbour.reshape(BLOCKS * 6)
    anywhere = pl.BlockSpec(memory_space=pl.ANY)
    scalars = pl.BlockSpec(memory_space=pltpu.SMEM)
    vector = pl.BlockSpec(memory_space=pltpu.VMEM)
    padded = (TILES, PITCH, LANES)
    plain = (TILES, 64, LANES)
    sides = (24, 64, LANES)
    tables = [pltpu.VMEM((20, *FACE), F32)] * 4
    dma = pltpu.SemaphoreType.DMA
    stage, got, got_layers, got_marks = pl.pallas_call(
        own_kernel,
        out_shape=[
            pltpu.VMEM((BLOCKS, *plain), F32),
            pltpu.VMEM((2, *padded), F32),
            pltpu.VMEM((2, 2, 6, *FACE), F32),
            pltpu.VMEM((2, 8, LANES), F32),
        ],
        in_specs=[anywhere, scalars, scalars, scalars],
        out_specs=[vector] * 4,
        scratch_shapes=[
            *[pltpu.VMEM((BLOCKS, *padded), F32)] * 3,
            pltpu.VMEM((BLOCKS, *sides), F32),
            pltpu.VMEM((2, *plain), F32),
            *tables,
            *[pltpu.VMEM((2, 4, *FACE), F32)] * 4,
            pltpu.VMEM((2, 2, 6, *FACE), F32),
            pltpu.VMEM((2, 8, LANES), F32),
            pltpu.SMEM((BLOCKS * 6,), jnp.int32),
            dma((BLOCKS, SLABS)),
            dma((2, 2)),
            dma((2, 2)),
            dma((2, SLABS)),
            dma((2, SLABS)),
            dma((2, 2)),
            dma((2, 2)),
        ],
        compiler_params=pltpu.CompilerParams(
            collective_id=0, has_side_effects=True, vmem_limit_bytes=48 << 20
        ),
    )(tiles, links, new_owner, new_slot)
    out = pl.pallas_call(
        layout_kernel,
        out_shape=jax.ShapeDtypeStruct((BLOCKS, SLABS, 32, 8, LANES), F32),
        in_specs=[vector] * 4 + [scalars] * 2,
        out_specs=anywhere,
        scratch_shapes=[
            *[pltpu.VMEM(padded, F32)] * 4,
            pltpu.VMEM(sides, F32),
            pltpu.VMEM((2, *plain), F32),
            pltpu.VMEM((SLABS, 32, 8, LANES), F32),
            dma((BLOCKS, SLABS)),
            dma((BLOCKS,)),
            dma((2, SLABS)),
        ],
        compiler_params=pltpu.CompilerParams(vmem_limit_bytes=16 << 20),
    )(stage, got, got_layers, got_marks, new_owner, new_slot)
    return out.transpose(0, 1, 3, 2, 4).reshape(concentration.shape)


def solution(mesh):
    return jax.shard_map(
        per_device,
        mesh=mesh,
        in_specs=(P(AXES, None, None), P(AXES, None), P(AXES), P(AXES)),
        out_specs=P(AXES, None, None),
        check_vma=False,
    )
```

```python
import jax
import jax.numpy as jnp
from jax import lax
from jax.experimental import pallas as pl
from jax.experimental.pallas import tpu as pltpu
from jax.sharding import PartitionSpec as P

MESH = pl.DeviceIdType.MESH
AXES = ("gx", "gy")
BLOCKS = 8
LANES = 128
TILES = 32
SLABS = 8
TOP = 8
PITCH = 80
F32 = jnp.float32
FACE = (32, LANES)
HALF = 4
FIRST, SECOND = 2, 5
STEP = 2


def masks_of():
    lane = lax.broadcasted_iota(jnp.int32, (8, LANES), 1)
    xc, yc = lane & 15, lane >> 4
    return {
        "xc": xc,
        "yc": yc,
        "x_first": xc == 0,
        "x_last": xc == 15,
        "y_first": yc == 0,
        "y_last": yc == 7,
    }


def turned(tile, shift):
    if isinstance(shift, int):
        shift %= LANES
        if shift == 0:
            return tile
    return pltpu.roll(tile, shift, 1)


def mobility(values):
    square = values - values * values
    return 0.00075 + 0.04 * (square * square)


def slab(z, offset=0):
    if offset:
        return pl.ds(TOP + 8 * z + offset, 8)
    return pl.ds(pl.multiple_of(TOP + 8 * z, 8), 8)


def eight(z):
    return pl.ds(pl.multiple_of(8 * z, 8), 8)


def part(k):
    return pl.ds(8 * k, 8)


def rows_of(block):
    return block.reshape(TILES * PITCH, LANES)


def z_rows(block, row):
    return rows_of(block)[pl.ds(row, TILES, stride=PITCH), :]


def set_z_rows(block, row, values):
    rows_of(block)[pl.ds(row, TILES, stride=PITCH), :] = values


def shifted_sides(masks, block, z, halo):
    rows = slab(z)
    sides = []
    for yf in range(8):
        own = turned(block[yf, rows, :], -1)
        sides.append(jnp.where(masks["x_last"], halo(0, yf), own))
    for yf in range(8):
        own = turned(block[24 + yf, rows, :], 1)
        sides.append(jnp.where(masks["x_first"], halo(1, yf), own))
    for xf in range(4):
        own = turned(block[8 * xf, rows, :], -16)
        sides.append(jnp.where(masks["y_last"], halo(2, xf), own))
    for xf in range(4):
        own = turned(block[8 * xf + 7, rows, :], 16)
        sides.append(jnp.where(masks["y_first"], halo(3, xf), own))
    return sides


def near(block, z, sides, xf, yf):
    rows, tile = slab(z), 8 * xf + yf
    return (
        block[tile + 8, rows, :] if xf < 3 else sides[yf],
        block[tile - 8, rows, :] if xf > 0 else sides[8 + yf],
        block[tile + 1, rows, :] if yf < 7 else sides[16 + xf],
        block[tile - 1, rows, :] if yf > 0 else sides[20 + xf],
        block[tile, slab(z, 1), :],
        block[tile, slab(z, -1), :],
    )


def chemical_slab(masks, field, chem, side_mobility, z, halo):
    sides = shifted_sides(masks, field, z, halo)
    for k, values in enumerate(sides):
        side_mobility[k, eight(z), :] = mobility(values)
    rows = slab(z)
    for xf in range(4):
        for yf in range(8):
            tile = field[8 * xf + yf, rows, :]
            a, b, c, d, e, f = near(field, z, sides, xf, yf)
            total = ((a + b) + (c + d)) + (e + f)
            value = tile * (14.0 + tile * (4.0 * tile - 6.0)) - (total + total)
            chem[8 * xf + yf, rows, :] = value


def advance_slab(masks, field, chem, scaled, side_mobility, out, z, halo):
    sides = shifted_sides(masks, chem, z, halo)
    side_scaled = [side_mobility[k, eight(z), :] for k in range(24)]
    rows = slab(z)
    for xf in range(4):
        for yf in range(8):
            tile = 8 * xf + yf
            u, m = chem[tile, rows, :], scaled[tile, rows, :]
            flux = None
            for u_near, m_near in zip(near(chem, z, sides, xf, yf), near(scaled, z, side_scaled, xf, yf)):
                term = (m + m_near) * (u_near - u)
                flux = term if flux is None else flux + term
            out[tile, rows, :] = field[tile, rows, :] + flux


def y_faces(masks, block):
    faces = []
    for yf in (0, 7):
        parts = []
        for xf in range(4):
            held = jnp.zeros((8, LANES), F32)
            for z in range(SLABS):
                tile = block[8 * xf + yf, slab(z), :]
                held = jnp.where(masks["yc"] == z, turned(tile, (z - yf) * 16), held)
            parts.append(held)
        faces.append(jnp.concatenate(parts, 0))
    return faces


def add_y(masks, block, d, change):
    yf = 7 if d == 2 else 0
    where = masks["y_last" if d == 2 else "y_first"]
    for xf in range(4):
        for z in range(SLABS):
            spread = turned(change[8 * xf : 8 * xf + 8], (yf - z) * 16)
            tile = 8 * xf + yf
            block[tile, slab(z), :] = block[tile, slab(z), :] + jnp.where(where, spread, 0.0)


def add_z(block, d, change):
    row = TOP + 63 if d == 4 else TOP
    set_z_rows(block, row, z_rows(block, row) + change)


def y_halo(face, side, xf, z):
    place = 7 if side == 2 else 0
    return turned(face[part(xf), :], lax.rem((place - z) * 16 + LANES, LANES))


def x_halo(face, side, yf, z):
    place = 15 if side == 0 else 0
    spot = (yf & 1) * 8 + z
    return turned(face[part(yf >> 1), :], lax.rem(place - spot + LANES, LANES))


def group_in(stage, xf, pair):
    rows = [stage[4 * yc + pair, pl.ds(xf, 16, stride=4), :] for yc in range(8)]
    return jnp.concatenate(rows, 0).T


def group_out(stage, xf, pair, block):
    tile = 8 * xf + 2 * pair
    both = jnp.concatenate([block[tile, TOP : TOP + 64, :], block[tile + 1, TOP : TOP + 64, :]], 0).T
    for yc in range(8):
        stage[4 * yc + pair, pl.ds(xf, 16, stride=4), :] = both[16 * yc : 16 * yc + 16]


def place():
    size = lax.axis_size(AXES)
    minor = lax.axis_size("gy")
    me = lax.axis_index("gx") * minor + lax.axis_index("gy")
    upper, lower = lax.rem(me + 1, size), lax.rem(me + size - 1, size)

    def coordinates(device):
        return (device // minor, lax.rem(device, minor))

    return me, coordinates(upper), coordinates(lower)


def remote(source, target, send, receive, device):
    return pltpu.make_async_remote_copy(
        source, target, send, receive, device_id=device, device_id_type=MESH
    )


def own_kernel(
    c_hbm, links, owner, slot, stage, got, got_layers, got_marks,
    field, chem, scaled, side_mobility, pay, y_c, z_c, y_u, z_u, sent_c, sent_u, came_c, came_u, packed, marks, table, local, remote_face,
    load_sem, face_send, face_recv, block_send, block_recv, pack_send, pack_recv,
):
    me, upper, lower = place()
    masks = masks_of()

    def load(b, xo):
        return pltpu.make_async_copy(c_hbm.at[b, xo], stage.at[b, :, eight(xo), :], load_sem.at[b, xo])

    @pl.loop(0, BLOCKS * SLABS)
    def _(i):
        load(i // SLABS, i % SLABS).start()

    barrier = pltpu.get_barrier_semaphore()
    for device in (upper, lower):
        pl.semaphore_signal(barrier, inc=1, device_id=device, device_id_type=MESH)

    def link(b, d):
        return links[b, d]

    near_base = {2: 0, 3: 8, 4: 0, 5: 8}
    far_base = {2: 18, 3: 16, 4: 16, 5: 18}
    own_base = {2: 8, 3: 0, 4: 8, 5: 0}
    picks = {}
    for d in (2, 3, 4, 5):
        least, first, second = jnp.int32(BLOCKS), jnp.int32(BLOCKS - 1), jnp.int32(0)
        for b in range(BLOCKS):
            p = link(b, d)
            far = (p >= 0) & ((p >> 3) != me)
            least = jnp.where(far, jnp.minimum(least, p & 7), least)
            first = jnp.where(far, jnp.minimum(first, b), first)
            second = jnp.where(far, b, second)
        picks[d] = (first + own_base[d], second + own_base[d])
        for b in range(BLOCKS):
            p = link(b, d)
            far = far_base[d] + ((p & 7) > least).astype(jnp.int32)
            own, near = own_base[d] + b, near_base[d] + (p & 7)
            here = (p >> 3) == me
            table[b * 6 + d] = jnp.where(p < 0, own, jnp.where(here, near, far))
            local[b * 6 + d] = jnp.where((p >= 0) & here, near, own)
            remote_face[b * 6 + d] = jnp.where((p >= 0) & ~here, far, own)
    moving, mark_right, mark_left = jnp.int32(0), jnp.int32(0), jnp.int32(0)
    for b in range(BLOCKS):
        goes_right, goes_left = owner[b] == me + 1, owner[b] == me - 1
        moving = jnp.where(goes_right, b, moving)
        mark_right = jnp.where(goes_right, slot[b] + 1, mark_right)
        mark_left = jnp.where((owner[b] >= 0) & goes_left, slot[b] + 1, mark_left)
    marks[0] = jnp.full((8, LANES), mark_right, jnp.int32).astype(F32)
    marks[1] = jnp.full((8, LANES), mark_left, jnp.int32).astype(F32)

    def take_in(b, xf, pair, extra=None):
        both = group_in(stage.at[b], xf, pair)
        for h in range(2):
            tile, values = 8 * xf + 2 * pair + h, both[64 * h : 64 * h + 64]
            if extra is None:
                field[b, tile, TOP : TOP + 64, :] = values
                scaled[b, tile, TOP : TOP + 64, :] = mobility(values)
            else:
                pay[extra, tile] = values

    def take_blocks(start, end):
        @pl.loop(start, end)
        def _(b):
            @pl.loop(0, 8)
            def _(k):
                for q in range(2):
                    take_in(b, k // 2, (k % 2) * 2 + q)

    @pl.loop(0, BLOCKS * SLABS)
    def _(i):
        load(i // SLABS, i % SLABS).wait()

    @pl.loop(0, 8)
    def _(k):
        for q in range(2):
            take_in(moving, k // 2, (k % 2) * 2 + q, 0)

    take_blocks(0, HALF)

    @pl.loop(0, TILES)
    def _(t):
        pay[1, t] = field[0, t, TOP : TOP + 64, :]

    pl.semaphore_wait(barrier, 2)

    def block_copies(z):
        return [
            remote(
                pay.at[side, :, eight(z), :], got.at[side, :, slab(z), :],
                block_send.at[side, z], block_recv.at[side, z], device,
            )
            for side, device in enumerate((upper, lower))
        ]

    def hand_on(start, end):
        for z in range(start, end):
            for copy in block_copies(z):
                copy.start()

    hand_on(0, FIRST)
    take_blocks(HALF, BLOCKS)

    def faces_of(values, y_table, z_table):
        @pl.loop(0, BLOCKS)
        def _(b):
            z_table[b] = z_rows(values.at[b], TOP)
            z_table[BLOCKS + b] = z_rows(values.at[b], TOP + 63)
            y_table[b], y_table[BLOCKS + b] = y_faces(masks, values.at[b])

    faces_of(field, y_c, z_c)

    def fill(message, y_table, z_table):
        for side, (y_dir, z_dir) in enumerate(((2, 5), (3, 4))):
            for k in range(2):
                message[side, k] = y_table[picks[y_dir][k]]
                message[side, 2 + k] = z_table[picks[z_dir][k]]

    def face_copies(k, message, came):
        return [
            remote(message.at[side], came.at[side], face_send.at[k, side], face_recv.at[k, side], device)
            for side, device in enumerate((upper, lower))
        ]

    def take(came, y_table, z_table):
        for side in range(2):
            for k in range(2):
                y_table[16 + 2 * side + k] = came[side, k]
                z_table[16 + 2 * side + k] = came[side, 2 + k]

    def halo_of(values, y_table, b, z):
        rows = slab(z)
        open_high, open_low = link(b, 0) < 0, link(b, 1) < 0
        high = jnp.where(open_high, b, link(b, 0) & 7)
        low = jnp.where(open_low, b, link(b, 1) & 7)

        def halo(side, k):
            if side == 0:
                return jnp.where(open_high, values[b, 24 + k, rows, :], turned(values[high, k, rows, :], 15))
            if side == 1:
                return jnp.where(open_low, values[b, k, rows, :], turned(values[low, 24 + k, rows, :], -15))
            return y_halo(y_table.at[local[b * 6 + side]], side, k, z)

        return halo

    def set_z(values, z_table, b, scale=None):
        for row, d in ((TOP + 64, 4), (TOP - 1, 5)):
            layer = z_table[local[b * 6 + d]]
            set_z_rows(values.at[b], row, layer)
            if scale is not None:
                set_z_rows(scale.at[b], row, mobility(layer))

    fill(sent_c, y_c, z_c)
    first_faces = face_copies(0, sent_c, came_c)
    for copy in first_faces:
        copy.start()
    hand_on(FIRST, SECOND)

    @pl.loop(0, BLOCKS)
    def _(b):
        set_z(field, z_c, b, scaled)

    @pl.loop(0, BLOCKS * SLABS // STEP)
    def _(i):
        b = i // (SLABS // STEP)
        for q in range(STEP):
            z = i % (SLABS // STEP) * STEP + q
            chemical_slab(masks, field.at[b], chem.at[b], side_mobility.at[b], z, halo_of(field, y_c, b, z))

    for copy in first_faces:
        copy.wait_recv()
    take(came_c, y_c, z_c)

    @pl.loop(0, BLOCKS)
    def _(b):
        for d in (2, 3):
            own = y_c[own_base[d] + b]
            add_y(masks, chem.at[b], d, -2.0 * (y_c[remote_face[b * 6 + d]] - own))
        for d in (4, 5):
            own = z_c[own_base[d] + b]
            add_z(chem.at[b], d, -2.0 * (z_c[remote_face[b * 6 + d]] - own))

    faces_of(chem, y_u, z_u)
    fill(sent_u, y_u, z_u)
    second_faces = face_copies(1, sent_u, came_u)
    for copy in second_faces:
        copy.start()
    hand_on(SECOND, SLABS)

    def pack(k, values, y_table, z_table):
        for side, b in ((0, moving), (1, 0)):
            for d in (2, 3):
                packed[side, k, d] = y_table[table[b * 6 + d]]
            for d in (4, 5):
                packed[side, k, d] = z_table[table[b * 6 + d]]

            @pl.loop(0, SLABS)
            def _(z, side=side, b=b):
                halo = halo_of(values, y_table, b, z)
                for d in range(2):
                    for yf in range(8):
                        spot = (yf & 1) * 8 + z
                        shift = lax.rem(spot - (0 if d else 15) + LANES, LANES)
                        held = packed[side, k, d, part(yf >> 1), :]
                        packed[side, k, d, part(yf >> 1), :] = jnp.where(
                            masks["xc"] == spot, turned(halo(d, yf), shift), held
                        )

    pack(0, field, y_c, z_c)

    @pl.loop(0, BLOCKS)
    def _(b):
        set_z(chem, z_u, b)

    @pl.loop(0, BLOCKS * SLABS // STEP)
    def _(i):
        b = i // (SLABS // STEP)
        for q in range(STEP):
            z = i % (SLABS // STEP) * STEP + q
            advance_slab(
                masks, field.at[b], chem.at[b], scaled.at[b], side_mobility.at[b], field.at[b], z,
                halo_of(chem, y_u, b, z),
            )

    for copy in second_faces:
        copy.wait_recv()
    take(came_u, y_u, z_u)
    pack(1, chem, y_u, z_u)
    pack_copies = []
    for side, device in enumerate((upper, lower)):
        pack_copies.append(
            remote(packed.at[side], got_layers.at[side], pack_send.at[0, side], pack_recv.at[0, side], device)
        )
        pack_copies.append(
            remote(marks.at[side], got_marks.at[side], pack_send.at[1, side], pack_recv.at[1, side], device)
        )
    for copy in pack_copies:
        copy.start()

    def far_flux(field_table, chem_table, b, d):
        own, far = own_base[d] + b, remote_face[b * 6 + d]
        passing = mobility(field_table[own]) + mobility(field_table[far])
        return passing * (chem_table[far] - chem_table[own])

    @pl.loop(0, BLOCKS)
    def _(b):
        for d in (2, 3):
            add_y(masks, field.at[b], d, far_flux(y_c, y_u, b, d))
        for d in (4, 5):
            add_z(field.at[b], d, far_flux(z_c, z_u, b, d))

    @pl.loop(0, BLOCKS * 8)
    def _(i):
        b, k = i // 8, i % 8
        for q in range(2):
            group_out(stage.at[b], k // 2, (k % 2) * 2 + q, field.at[b])

    for copy in pack_copies:
        copy.wait()
    for z in range(SLABS):
        for copy in block_copies(z):
            copy.wait()
    for copy in first_faces + second_faces:
        copy.wait_send()


def layout_kernel(
    stage, got, got_layers, got_marks, owner, slot, out,
    arrived, scaled, chem, stepped, side_mobility, final, zeros, keep_sem, zero_sem, new_sem,
):
    me, _, _ = place()
    masks = masks_of()

    def keep_copy(b, xo):
        return pltpu.make_async_copy(stage.at[b, :, 8 * xo : 8 * xo + 8, :], out.at[slot[b], xo], keep_sem.at[b, xo])

    def new_copy(side, xo):
        return pltpu.make_async_copy(
            final.at[side, :, 8 * xo : 8 * xo + 8, :], out.at[places[side] - 1, xo], new_sem.at[side, xo]
        )

    kept = jnp.int32(0)
    for b in range(BLOCKS):
        stays = owner[b] == me
        kept = kept + stays.astype(jnp.int32)

        @pl.when(stays)
        def _(b=b):
            for xo in range(SLABS):
                keep_copy(b, xo).start()

    places = [jnp.max(got_marks[side]).astype(jnp.int32) for side in range(2)]
    count = kept
    for target in places:
        count = count + (target > 0).astype(jnp.int32)
    zeros[...] = jnp.zeros_like(zeros)
    for s in range(BLOCKS):

        @pl.when(s >= count)
        def _(s=s):
            pltpu.make_async_copy(zeros, out.at[s], zero_sem.at[s]).start()

    for side in range(2):

        @pl.when(places[side] > 0)
        def _(side=side):
            layers = got_layers.at[side]

            def halo_of(k, z):
                def halo(d, f):
                    return (x_halo if d < 2 else y_halo)(layers.at[k, d], d, f, z)

                return halo

            @pl.loop(0, SLABS)
            def _(z):
                rows = slab(z)
                for t in range(TILES):
                    values = got[side, t, rows, :]
                    arrived[t, rows, :] = values
                    scaled[t, rows, :] = mobility(values)

            for row, d in ((TOP + 64, 4), (TOP - 1, 5)):
                set_z_rows(arrived, row, layers[0, d])
                set_z_rows(scaled, row, mobility(layers[0, d]))
                set_z_rows(chem, row, layers[1, d])

            @pl.loop(0, SLABS)
            def _(z):
                chemical_slab(masks, arrived, chem, side_mobility, z, halo_of(0, z))

            @pl.loop(0, SLABS)
            def _(z):
                advance_slab(masks, arrived, chem, scaled, side_mobility, stepped, z, halo_of(1, z))

            @pl.loop(0, 8)
            def _(k):
                for q in range(2):
                    group_out(final.at[side], k // 2, (k % 2) * 2 + q, stepped)

            for xo in range(SLABS):
                new_copy(side, xo).start()

    for b in range(BLOCKS):

        @pl.when(owner[b] == me)
        def _(b=b):
            for xo in range(SLABS):
                keep_copy(b, xo).wait()

    for s in range(BLOCKS):

        @pl.when(s >= count)
        def _(s=s):
            pltpu.make_async_copy(zeros, out.at[s], zero_sem.at[s]).wait()

    for side in range(2):

        @pl.when(places[side] > 0)
        def _(side=side):
            for xo in range(SLABS):
                new_copy(side, xo).wait()


def per_device(concentration, neighbour, new_owner, new_slot):
    tiles = concentration.reshape(BLOCKS, SLABS, 8, 32, LANES).transpose(0, 1, 3, 2, 4)
    anywhere = pl.BlockSpec(memory_space=pl.ANY)
    scalars = pl.BlockSpec(memory_space=pltpu.SMEM)
    vector = pl.BlockSpec(memory_space=pltpu.VMEM)
    padded = (TILES, PITCH, LANES)
    plain = (TILES, 64, LANES)
    sides = (24, 64, LANES)
    tables = [pltpu.VMEM((20, *FACE), F32)] * 4
    dma = pltpu.SemaphoreType.DMA
    stage, got, got_layers, got_marks = pl.pallas_call(
        own_kernel,
        out_shape=[
            pltpu.VMEM((BLOCKS, *plain), F32),
            pltpu.VMEM((2, *padded), F32),
            pltpu.VMEM((2, 2, 6, *FACE), F32),
            pltpu.VMEM((2, 8, LANES), F32),
        ],
        in_specs=[anywhere, scalars, scalars, scalars],
        out_specs=[vector] * 4,
        scratch_shapes=[
            *[pltpu.VMEM((BLOCKS, *padded), F32)] * 3,
            pltpu.VMEM((BLOCKS, *sides), F32),
            pltpu.VMEM((2, *plain), F32),
            *tables,
            *[pltpu.VMEM((2, 4, *FACE), F32)] * 4,
            pltpu.VMEM((2, 2, 6, *FACE), F32),
            pltpu.VMEM((2, 8, LANES), F32),
            *[pltpu.SMEM((BLOCKS * 6,), jnp.int32)] * 3,
            dma((BLOCKS, SLABS)),
            dma((2, 2)),
            dma((2, 2)),
            dma((2, SLABS)),
            dma((2, SLABS)),
            dma((2, 2)),
            dma((2, 2)),
        ],
        compiler_params=pltpu.CompilerParams(
            collective_id=0, has_side_effects=True, vmem_limit_bytes=48 << 20
        ),
    )(tiles, neighbour, new_owner, new_slot)
    out = pl.pallas_call(
        layout_kernel,
        out_shape=jax.ShapeDtypeStruct((BLOCKS, SLABS, 32, 8, LANES), F32),
        in_specs=[vector] * 4 + [scalars] * 2,
        out_specs=anywhere,
        scratch_shapes=[
            *[pltpu.VMEM(padded, F32)] * 4,
            pltpu.VMEM(sides, F32),
            pltpu.VMEM((2, *plain), F32),
            pltpu.VMEM((SLABS, 32, 8, LANES), F32),
            dma((BLOCKS, SLABS)),
            dma((BLOCKS,)),
            dma((2, SLABS)),
        ],
        compiler_params=pltpu.CompilerParams(vmem_limit_bytes=16 << 20),
    )(stage, got, got_layers, got_marks, new_owner, new_slot)
    return out.transpose(0, 1, 3, 2, 4).reshape(concentration.shape)


def solution(mesh):
    return jax.shard_map(
        per_device,
        mesh=mesh,
        in_specs=(P(AXES, None, None), P(AXES, None), P(AXES), P(AXES)),
        out_specs=P(AXES, None, None),
        check_vma=False,
    )
```

```python
import jax
import jax.numpy as jnp
from jax import lax
from jax.experimental import pallas as pl
from jax.experimental.pallas import tpu as pltpu
from jax.sharding import PartitionSpec as P

MESH = pl.DeviceIdType.MESH
AXES = ("gx", "gy")
BLOCKS = 8
LANES = 128
TILES = 32
SLABS = 8
TOP = 8
PITCH = 80
F32 = jnp.float32
FACE = (32, LANES)
FIRST, SECOND = 3, 6
STEP = 4


def masks_of():
    lane = lax.broadcasted_iota(jnp.int32, (8, LANES), 1)
    xc, yc = lane & 15, lane >> 4
    return {
        "xc": xc,
        "yc": yc,
        "x_first": xc == 0,
        "x_last": xc == 15,
        "y_first": yc == 0,
        "y_last": yc == 7,
    }


def turned(tile, shift):
    if isinstance(shift, int):
        shift %= LANES
        if shift == 0:
            return tile
    return pltpu.roll(tile, shift, 1)


def mobility(values):
    square = values - values * values
    return 0.00075 + 0.04 * (square * square)


def slab(z, offset=0):
    if offset:
        return pl.ds(TOP + 8 * z + offset, 8)
    return pl.ds(TOP + 8 * z if isinstance(z, int) else pl.multiple_of(TOP + 8 * z, 8), 8)


def eight(z):
    return pl.ds(pl.multiple_of(8 * z, 8), 8)


def part(k):
    return pl.ds(8 * k, 8)


def rows_of(block):
    return block.reshape(TILES * PITCH, LANES)


def z_rows(block, row):
    return rows_of(block)[pl.ds(row, TILES, stride=PITCH), :]


def set_z_rows(block, row, values):
    rows_of(block)[pl.ds(row, TILES, stride=PITCH), :] = values


def shifted_sides(masks, block, z, halo):
    rows = slab(z)
    sides = []
    for yf in range(8):
        own = turned(block[yf, rows, :], -1)
        sides.append(jnp.where(masks["x_last"], halo(0, yf), own))
    for yf in range(8):
        own = turned(block[24 + yf, rows, :], 1)
        sides.append(jnp.where(masks["x_first"], halo(1, yf), own))
    for xf in range(4):
        own = turned(block[8 * xf, rows, :], -16)
        sides.append(jnp.where(masks["y_last"], halo(2, xf), own))
    for xf in range(4):
        own = turned(block[8 * xf + 7, rows, :], 16)
        sides.append(jnp.where(masks["y_first"], halo(3, xf), own))
    return sides


def near(block, z, sides, xf, yf):
    rows, tile = slab(z), 8 * xf + yf
    return (
        block[tile + 8, rows, :] if xf < 3 else sides[yf],
        block[tile - 8, rows, :] if xf > 0 else sides[8 + yf],
        block[tile + 1, rows, :] if yf < 7 else sides[16 + xf],
        block[tile - 1, rows, :] if yf > 0 else sides[20 + xf],
        block[tile, slab(z, 1), :],
        block[tile, slab(z, -1), :],
    )


def chemical_slab(masks, field, chem, side_mobility, z, halo):
    sides = shifted_sides(masks, field, z, halo)
    for k, values in enumerate(sides):
        side_mobility[k, eight(z), :] = mobility(values)
    rows = slab(z)
    for xf in range(4):
        for yf in range(8):
            tile = field[8 * xf + yf, rows, :]
            a, b, c, d, e, f = near(field, z, sides, xf, yf)
            total = ((a + b) + (c + d)) + (e + f)
            value = tile * (14.0 + tile * (4.0 * tile - 6.0)) - (total + total)
            chem[8 * xf + yf, rows, :] = value


def advance_slab(masks, field, chem, scaled, side_mobility, out, z, halo):
    sides = shifted_sides(masks, chem, z, halo)
    side_scaled = [side_mobility[k, eight(z), :] for k in range(24)]
    rows = slab(z)
    for xf in range(4):
        for yf in range(8):
            tile = 8 * xf + yf
            u, m = chem[tile, rows, :], scaled[tile, rows, :]
            flux = None
            for u_near, m_near in zip(near(chem, z, sides, xf, yf), near(scaled, z, side_scaled, xf, yf)):
                term = (m + m_near) * (u_near - u)
                flux = term if flux is None else flux + term
            out[tile, rows, :] = field[tile, rows, :] + flux


def y_faces(masks, block):
    faces = []
    for yf in (0, 7):
        parts = []
        for xf in range(4):
            held = jnp.zeros((8, LANES), F32)
            for z in range(SLABS):
                tile = block[8 * xf + yf, slab(z), :]
                held = jnp.where(masks["yc"] == z, turned(tile, (z - yf) * 16), held)
            parts.append(held)
        faces.append(jnp.concatenate(parts, 0))
    return faces


def add_y(masks, block, d, change):
    yf = 7 if d == 2 else 0
    where = masks["y_last" if d == 2 else "y_first"]
    for xf in range(4):
        for z in range(SLABS):
            spread = turned(change[8 * xf : 8 * xf + 8], (yf - z) * 16)
            tile = 8 * xf + yf
            block[tile, slab(z), :] = block[tile, slab(z), :] + jnp.where(where, spread, 0.0)


def add_z(block, d, change):
    row = TOP + 63 if d == 4 else TOP
    set_z_rows(block, row, z_rows(block, row) + change)


def y_halo(face, side, xf, z):
    place = 7 if side == 2 else 0
    return turned(face[part(xf), :], lax.rem((place - z) * 16 + LANES, LANES))


def x_halo(face, side, yf, z):
    place = 15 if side == 0 else 0
    spot = (yf & 1) * 8 + z
    return turned(face[part(yf >> 1), :], lax.rem(place - spot + LANES, LANES))


def group_in(stage, xf, pair):
    rows = [stage[4 * yc + pair, pl.ds(xf, 16, stride=4), :] for yc in range(8)]
    return jnp.concatenate(rows, 0).T


def group_out(stage, xf, pair, block):
    tile = 8 * xf + 2 * pair
    both = jnp.concatenate([block[tile, TOP : TOP + 64, :], block[tile + 1, TOP : TOP + 64, :]], 0).T
    for yc in range(8):
        stage[4 * yc + pair, pl.ds(xf, 16, stride=4), :] = both[16 * yc : 16 * yc + 16]


def place():
    size = lax.axis_size(AXES)
    minor = lax.axis_size("gy")
    me = lax.axis_index("gx") * minor + lax.axis_index("gy")
    upper, lower = lax.rem(me + 1, size), lax.rem(me + size - 1, size)

    def coordinates(device):
        return (device // minor, lax.rem(device, minor))

    return size, me, coordinates(upper), coordinates(lower)


def remote(source, target, send, receive, device):
    return pltpu.make_async_remote_copy(
        source, target, send, receive, device_id=device, device_id_type=MESH
    )


def own_kernel(
    c_hbm, links, owner, slot, stage, got, got_layers, got_marks,
    field, chem, scaled, side_mobility, pay, y_c, z_c, y_u, z_u, sent_c, sent_u, came_c, came_u, packed, marks, table, local, remote_face,
    load_sem, face_send, face_recv, block_send, block_recv, pack_send, pack_recv, lower_here,
):
    size, me, upper, lower = place()
    masks = masks_of()

    def load(b, xo):
        return pltpu.make_async_copy(c_hbm.at[b, xo], stage.at[b, :, eight(xo), :], load_sem.at[b, xo])

    @pl.loop(0, BLOCKS * SLABS)
    def _(i):
        load(i // SLABS, i % SLABS).start()

    barrier = pltpu.get_barrier_semaphore()
    pl.semaphore_signal(barrier, inc=1, device_id=lower, device_id_type=MESH)

    def link(b, d):
        return links[b, d]

    near_base = {2: 0, 3: 8, 4: 0, 5: 8}
    far_base = {2: 18, 3: 16, 4: 16, 5: 18}
    own_base = {2: 8, 3: 0, 4: 8, 5: 0}
    picks = {}
    for d in (2, 3, 4, 5):
        least, first, second = jnp.int32(BLOCKS), jnp.int32(BLOCKS - 1), jnp.int32(0)
        for b in range(BLOCKS):
            p = link(b, d)
            far = (p >= 0) & ((p >> 3) != me)
            least = jnp.where(far, jnp.minimum(least, p & 7), least)
            first = jnp.where(far, jnp.minimum(first, b), first)
            second = jnp.where(far, b, second)
        picks[d] = (first + own_base[d], second + own_base[d])
        for b in range(BLOCKS):
            p = link(b, d)
            far = far_base[d] + ((p & 7) > least).astype(jnp.int32)
            own, near = own_base[d] + b, near_base[d] + (p & 7)
            here = (p >> 3) == me
            table[b * 6 + d] = jnp.where(p < 0, own, jnp.where(here, near, far))
            local[b * 6 + d] = jnp.where((p >= 0) & here, near, own)
            remote_face[b * 6 + d] = jnp.where((p >= 0) & ~here, far, own)
    moving, mark_right, mark_left = jnp.int32(0), jnp.int32(0), jnp.int32(0)
    for b in range(BLOCKS):
        goes_right, goes_left = owner[b] == me + 1, owner[b] == me - 1
        moving = jnp.where(goes_right, b, moving)
        mark_right = jnp.where(goes_right, slot[b] + 1, mark_right)
        mark_left = jnp.where((owner[b] >= 0) & goes_left, slot[b] + 1, mark_left)
    marks[0] = jnp.full((8, LANES), mark_right, jnp.int32).astype(F32)
    marks[1] = jnp.full((8, LANES), mark_left, jnp.int32).astype(F32)

    def take_in(b, xf, pair, extra=None):
        both = group_in(stage.at[b], xf, pair)
        for h in range(2):
            tile, values = 8 * xf + 2 * pair + h, both[64 * h : 64 * h + 64]
            if extra is None:
                field[b, tile, TOP : TOP + 64, :] = values
                scaled[b, tile, TOP : TOP + 64, :] = mobility(values)
            else:
                pay[extra, tile] = values

    def take_blocks(start, end):
        @pl.loop(start, end)
        def _(b):
            @pl.loop(0, 4)
            def _(k):
                for q in range(4):
                    take_in(b, k, q)

    def block_copy(side, z):
        return remote(
            pay.at[side, :, eight(z), :], got.at[side, :, slab(z), :],
            block_send.at[side, z], block_recv.at[side, z], (upper, lower)[side],
        )

    has_upper, has_lower = me < size - 1, me > 0

    def hand_on(side, start, end):
        @pl.when((has_upper, has_lower)[side])
        def _():
            for z in range(start, end):
                block_copy(side, z).start()

    @pl.loop(0, BLOCKS * SLABS)
    def _(i):
        load(i // SLABS, i % SLABS).wait()

    @pl.loop(0, 4)
    def _(k):
        for q in range(4):
            take_in(moving, k, q, 0)

    pl.semaphore_wait(barrier, 1)
    pl.semaphore_signal(lower_here, inc=1, device_id=upper, device_id_type=MESH)
    hand_on(0, 0, FIRST)
    take_blocks(0, 1)

    @pl.loop(0, TILES)
    def _(t):
        pay[1, t] = field[0, t, TOP : TOP + 64, :]

    @pl.when(has_lower)
    def _():
        pl.semaphore_wait(lower_here, 1)

    hand_on(1, 0, FIRST)
    take_blocks(1, BLOCKS)

    def faces_of(values, y_table, z_table):
        @pl.loop(0, BLOCKS)
        def _(b):
            z_table[b] = z_rows(values.at[b], TOP)
            z_table[BLOCKS + b] = z_rows(values.at[b], TOP + 63)
            y_table[b], y_table[BLOCKS + b] = y_faces(masks, values.at[b])

    faces_of(field, y_c, z_c)

    def fill(message, y_table, z_table):
        for side, (y_dir, z_dir) in enumerate(((2, 5), (3, 4))):
            for k in range(2):
                message[side, k] = y_table[picks[y_dir][k]]
                message[side, 2 + k] = z_table[picks[z_dir][k]]

    def face_copies(k, message, came):
        return [
            remote(message.at[side], came.at[side], face_send.at[k, side], face_recv.at[k, side], device)
            for side, device in enumerate((upper, lower))
        ]

    def take(came, y_table, z_table):
        for side in range(2):
            for k in range(2):
                y_table[16 + 2 * side + k] = came[side, k]
                z_table[16 + 2 * side + k] = came[side, 2 + k]

    def halo_of(values, y_table, b, z):
        rows = slab(z)
        open_high, open_low = link(b, 0) < 0, link(b, 1) < 0
        high = jnp.where(open_high, b, link(b, 0) & 7)
        low = jnp.where(open_low, b, link(b, 1) & 7)

        def halo(side, k):
            if side == 0:
                return jnp.where(open_high, values[b, 24 + k, rows, :], turned(values[high, k, rows, :], 15))
            if side == 1:
                return jnp.where(open_low, values[b, k, rows, :], turned(values[low, 24 + k, rows, :], -15))
            return y_halo(y_table.at[local[b * 6 + side]], side, k, z)

        return halo

    def set_z(values, z_table, b, scale=None):
        for row, d in ((TOP + 64, 4), (TOP - 1, 5)):
            layer = z_table[local[b * 6 + d]]
            set_z_rows(values.at[b], row, layer)
            if scale is not None:
                set_z_rows(scale.at[b], row, mobility(layer))

    fill(sent_c, y_c, z_c)

    @pl.when(me == 0)
    def _():
        pl.semaphore_wait(lower_here, 1)

    first_faces = face_copies(0, sent_c, came_c)
    for copy in first_faces:
        copy.start()
    for side in range(2):
        hand_on(side, FIRST, SECOND)

    @pl.loop(0, BLOCKS)
    def _(b):
        set_z(field, z_c, b, scaled)

    @pl.loop(0, BLOCKS * SLABS // STEP)
    def _(i):
        b = i // (SLABS // STEP)
        for q in range(STEP):
            z = i % (SLABS // STEP) * STEP + q
            chemical_slab(masks, field.at[b], chem.at[b], side_mobility.at[b], z, halo_of(field, y_c, b, z))

    for copy in first_faces:
        copy.wait_recv()
    take(came_c, y_c, z_c)

    @pl.loop(0, BLOCKS)
    def _(b):
        for d in (2, 3):
            own = y_c[own_base[d] + b]
            add_y(masks, chem.at[b], d, -2.0 * (y_c[remote_face[b * 6 + d]] - own))
        for d in (4, 5):
            own = z_c[own_base[d] + b]
            add_z(chem.at[b], d, -2.0 * (z_c[remote_face[b * 6 + d]] - own))

    faces_of(chem, y_u, z_u)
    fill(sent_u, y_u, z_u)
    second_faces = face_copies(1, sent_u, came_u)
    for copy in second_faces:
        copy.start()
    for side in range(2):
        hand_on(side, SECOND, SLABS)

    def pack(k, values, y_table, z_table):
        for side, b in ((0, moving), (1, 0)):
            for d in (2, 3):
                packed[side, k, d] = y_table[table[b * 6 + d]]
            for d in (4, 5):
                packed[side, k, d] = z_table[table[b * 6 + d]]

            for d in range(2):

                @pl.loop(0, 4)
                def _(v, side=side, b=b, d=d):
                    held = jnp.zeros((8, LANES), F32)
                    for z in range(SLABS):
                        halo = halo_of(values, y_table, b, z)
                        for e in range(2):
                            spot = 8 * e + z
                            moved = turned(halo(d, 2 * v + e), spot - (0 if d else 15))
                            held = jnp.where(masks["xc"] == spot, moved, held)
                    packed[side, k, d, eight(v), :] = held

    pack(0, field, y_c, z_c)

    @pl.loop(0, BLOCKS)
    def _(b):
        set_z(chem, z_u, b)

    @pl.loop(0, BLOCKS * SLABS // STEP)
    def _(i):
        b = i // (SLABS // STEP)
        for q in range(STEP):
            z = i % (SLABS // STEP) * STEP + q
            advance_slab(
                masks, field.at[b], chem.at[b], scaled.at[b], side_mobility.at[b], field.at[b], z,
                halo_of(chem, y_u, b, z),
            )

    for copy in second_faces:
        copy.wait_recv()
    take(came_u, y_u, z_u)
    pack(1, chem, y_u, z_u)

    def pack_copies(side):
        device = (upper, lower)[side]
        return [
            remote(packed.at[side], got_layers.at[side], pack_send.at[0, side], pack_recv.at[0, side], device),
            remote(marks.at[side], got_marks.at[side], pack_send.at[1, side], pack_recv.at[1, side], device),
        ]

    for side in range(2):

        @pl.when((has_upper, has_lower)[side])
        def _(side=side):
            for copy in pack_copies(side):
                copy.start()

    def far_flux(field_table, chem_table, b, d):
        own, far = own_base[d] + b, remote_face[b * 6 + d]
        passing = mobility(field_table[own]) + mobility(field_table[far])
        return passing * (chem_table[far] - chem_table[own])

    @pl.loop(0, BLOCKS)
    def _(b):
        for d in (2, 3):
            add_y(masks, field.at[b], d, far_flux(y_c, y_u, b, d))
        for d in (4, 5):
            add_z(field.at[b], d, far_flux(z_c, z_u, b, d))

    @pl.loop(0, BLOCKS * 4)
    def _(i):
        b, k = i // 4, i % 4
        for q in range(4):
            group_out(stage.at[b], k, q, field.at[b])

    for side in range(2):

        @pl.when((has_upper, has_lower)[side])
        def _(side=side):
            for copy in pack_copies(side) + [block_copy(side, z) for z in range(SLABS)]:
                copy.wait_send()

        @pl.when((has_lower, has_upper)[side])
        def _(side=side):
            for copy in pack_copies(side) + [block_copy(side, z) for z in range(SLABS)]:
                copy.wait_recv()

    for copy in first_faces + second_faces:
        copy.wait_send()


def layout_kernel(
    stage, got, got_layers, got_marks, owner, slot, out,
    arrived, scaled, chem, stepped, side_mobility, final, zeros, keep_sem, zero_sem, new_sem,
):
    size, me, _, _ = place()
    masks = masks_of()

    def keep_copy(b, xo):
        return pltpu.make_async_copy(stage.at[b, :, 8 * xo : 8 * xo + 8, :], out.at[slot[b], xo], keep_sem.at[b, xo])

    def new_copy(side, xo):
        return pltpu.make_async_copy(
            final.at[side, :, 8 * xo : 8 * xo + 8, :], out.at[places[side] - 1, xo], new_sem.at[side, xo]
        )

    kept = jnp.int32(0)
    for b in range(BLOCKS):
        stays = owner[b] == me
        kept = kept + stays.astype(jnp.int32)

        @pl.when(stays)
        def _(b=b):
            for xo in range(SLABS):
                keep_copy(b, xo).start()

    places = [
        jnp.where(there, jnp.max(got_marks[side]).astype(jnp.int32), 0)
        for side, there in enumerate((me > 0, me < size - 1))
    ]
    count = kept
    for target in places:
        count = count + (target > 0).astype(jnp.int32)
    zeros[...] = jnp.zeros_like(zeros)
    for s in range(BLOCKS):

        @pl.when(s >= count)
        def _(s=s):
            pltpu.make_async_copy(zeros, out.at[s], zero_sem.at[s]).start()

    for side in range(2):

        @pl.when(places[side] > 0)
        def _(side=side):
            layers = got_layers.at[side]

            def halo_of(k, z):
                def halo(d, f):
                    return (x_halo if d < 2 else y_halo)(layers.at[k, d], d, f, z)

                return halo

            @pl.loop(0, SLABS)
            def _(z):
                rows = slab(z)
                for t in range(TILES):
                    values = got[side, t, rows, :]
                    arrived[t, rows, :] = values
                    scaled[t, rows, :] = mobility(values)

            for row, d in ((TOP + 64, 4), (TOP - 1, 5)):
                set_z_rows(arrived, row, layers[0, d])
                set_z_rows(scaled, row, mobility(layers[0, d]))
                set_z_rows(chem, row, layers[1, d])

            @pl.loop(0, SLABS)
            def _(z):
                chemical_slab(masks, arrived, chem, side_mobility, z, halo_of(0, z))

            @pl.loop(0, SLABS)
            def _(z):
                advance_slab(masks, arrived, chem, scaled, side_mobility, stepped, z, halo_of(1, z))

            @pl.loop(0, 8)
            def _(k):
                for q in range(2):
                    group_out(final.at[side], k // 2, (k % 2) * 2 + q, stepped)

            for xo in range(SLABS):
                new_copy(side, xo).start()

    for b in range(BLOCKS):

        @pl.when(owner[b] == me)
        def _(b=b):
            for xo in range(SLABS):
                keep_copy(b, xo).wait()

    for s in range(BLOCKS):

        @pl.when(s >= count)
        def _(s=s):
            pltpu.make_async_copy(zeros, out.at[s], zero_sem.at[s]).wait()

    for side in range(2):

        @pl.when(places[side] > 0)
        def _(side=side):
            for xo in range(SLABS):
                new_copy(side, xo).wait()


def per_device(concentration, neighbour, new_owner, new_slot):
    tiles = concentration.reshape(BLOCKS, SLABS, 8, 32, LANES).transpose(0, 1, 3, 2, 4)
    anywhere = pl.BlockSpec(memory_space=pl.ANY)
    scalars = pl.BlockSpec(memory_space=pltpu.SMEM)
    vector = pl.BlockSpec(memory_space=pltpu.VMEM)
    padded = (TILES, PITCH, LANES)
    plain = (TILES, 64, LANES)
    sides = (24, 64, LANES)
    tables = [pltpu.VMEM((20, *FACE), F32)] * 4
    dma = pltpu.SemaphoreType.DMA
    stage, got, got_layers, got_marks = pl.pallas_call(
        own_kernel,
        out_shape=[
            pltpu.VMEM((BLOCKS, *plain), F32),
            pltpu.VMEM((2, *padded), F32),
            pltpu.VMEM((2, 2, 6, *FACE), F32),
            pltpu.VMEM((2, 8, LANES), F32),
        ],
        in_specs=[anywhere, scalars, scalars, scalars],
        out_specs=[vector] * 4,
        scratch_shapes=[
            *[pltpu.VMEM((BLOCKS, *padded), F32)] * 3,
            pltpu.VMEM((BLOCKS, *sides), F32),
            pltpu.VMEM((2, *plain), F32),
            *tables,
            *[pltpu.VMEM((2, 4, *FACE), F32)] * 4,
            pltpu.VMEM((2, 2, 6, *FACE), F32),
            pltpu.VMEM((2, 8, LANES), F32),
            *[pltpu.SMEM((BLOCKS * 6,), jnp.int32)] * 3,
            dma((BLOCKS, SLABS)),
            dma((2, 2)),
            dma((2, 2)),
            dma((2, SLABS)),
            dma((2, SLABS)),
            dma((2, 2)),
            dma((2, 2)),
            pltpu.SemaphoreType.REGULAR,
        ],
        compiler_params=pltpu.CompilerParams(
            collective_id=0, has_side_effects=True, vmem_limit_bytes=48 << 20
        ),
    )(tiles, neighbour, new_owner, new_slot)
    out = pl.pallas_call(
        layout_kernel,
        out_shape=jax.ShapeDtypeStruct((BLOCKS, SLABS, 32, 8, LANES), F32),
        in_specs=[vector] * 4 + [scalars] * 2,
        out_specs=anywhere,
        scratch_shapes=[
            *[pltpu.VMEM(padded, F32)] * 4,
            pltpu.VMEM(sides, F32),
            pltpu.VMEM((2, *plain), F32),
            pltpu.VMEM((SLABS, 32, 8, LANES), F32),
            dma((BLOCKS, SLABS)),
            dma((BLOCKS,)),
            dma((2, SLABS)),
        ],
        compiler_params=pltpu.CompilerParams(vmem_limit_bytes=16 << 20),
    )(stage, got, got_layers, got_marks, new_owner, new_slot)
    return out.transpose(0, 1, 3, 2, 4).reshape(concentration.shape)


def solution(mesh):
    return jax.shard_map(
        per_device,
        mesh=mesh,
        in_specs=(P(AXES, None, None), P(AXES, None), P(AXES), P(AXES)),
        out_specs=P(AXES, None, None),
        check_vma=False,
    )
```

```python
import jax
import jax.numpy as jnp
from jax import lax
from jax.experimental import pallas as pl
from jax.experimental.pallas import tpu as pltpu
from jax.sharding import PartitionSpec as P

MESH = pl.DeviceIdType.MESH
AXES = ("gx", "gy")
BLOCKS = 8
LANES = 128
TILES = 32
SLABS = 8
TOP = 8
PITCH = 80
F32 = jnp.float32
FACE = (32, LANES)
AFTER = (2, 3, 4, 5, 7, 8)
STEP = 4
SPLIT = 4


def masks_of():
    lane = lax.broadcasted_iota(jnp.int32, (8, LANES), 1)
    xc, yc = lane & 15, lane >> 4
    return {
        "xc": xc,
        "yc": yc,
        "x_first": xc == 0,
        "x_last": xc == 15,
        "y_first": yc == 0,
        "y_last": yc == 7,
    }


def turned(tile, shift):
    if isinstance(shift, int):
        shift %= LANES
        if shift == 0:
            return tile
    return pltpu.roll(tile, shift, 1)


def mobility(values):
    square = values - values * values
    return 0.00075 + 0.04 * (square * square)


def slab(z, offset=0):
    if offset:
        return pl.ds(TOP + 8 * z + offset, 8)
    return pl.ds(TOP + 8 * z if isinstance(z, int) else pl.multiple_of(TOP + 8 * z, 8), 8)


def eight(z):
    return pl.ds(pl.multiple_of(8 * z, 8), 8)


def part(k):
    return pl.ds(8 * k, 8)


def rows_of(block):
    return block.reshape(TILES * PITCH, LANES)


def z_rows(block, row):
    return rows_of(block)[pl.ds(row, TILES, stride=PITCH), :]


def set_z_rows(block, row, values):
    rows_of(block)[pl.ds(row, TILES, stride=PITCH), :] = values


def shifted_sides(masks, block, z, halo):
    rows = slab(z)
    sides = []
    for yf in range(8):
        own = turned(block[yf, rows, :], -1)
        sides.append(jnp.where(masks["x_last"], halo(0, yf), own))
    for yf in range(8):
        own = turned(block[24 + yf, rows, :], 1)
        sides.append(jnp.where(masks["x_first"], halo(1, yf), own))
    for xf in range(4):
        own = turned(block[8 * xf, rows, :], -16)
        sides.append(jnp.where(masks["y_last"], halo(2, xf), own))
    for xf in range(4):
        own = turned(block[8 * xf + 7, rows, :], 16)
        sides.append(jnp.where(masks["y_first"], halo(3, xf), own))
    return sides


def near(block, z, sides, xf, yf):
    rows, tile = slab(z), 8 * xf + yf
    return (
        block[tile + 8, rows, :] if xf < 3 else sides[yf],
        block[tile - 8, rows, :] if xf > 0 else sides[8 + yf],
        block[tile + 1, rows, :] if yf < 7 else sides[16 + xf],
        block[tile - 1, rows, :] if yf > 0 else sides[20 + xf],
        block[tile, slab(z, 1), :],
        block[tile, slab(z, -1), :],
    )


def chemical_slab(masks, field, chem, side_mobility, z, halo):
    sides = shifted_sides(masks, field, z, halo)
    for k, values in enumerate(sides):
        side_mobility[k, eight(z), :] = mobility(values)
    rows = slab(z)
    for xf in range(4):
        for yf in range(8):
            tile = field[8 * xf + yf, rows, :]
            a, b, c, d, e, f = near(field, z, sides, xf, yf)
            total = ((a + b) + (c + d)) + (e + f)
            value = tile * (14.0 + tile * (4.0 * tile - 6.0)) - (total + total)
            chem[8 * xf + yf, rows, :] = value


def advance_slab(masks, field, chem, scaled, side_mobility, out, z, halo):
    sides = shifted_sides(masks, chem, z, halo)
    side_scaled = [side_mobility[k, eight(z), :] for k in range(24)]
    rows = slab(z)
    for xf in range(4):
        for yf in range(8):
            tile = 8 * xf + yf
            u, m = chem[tile, rows, :], scaled[tile, rows, :]
            flux = None
            for u_near, m_near in zip(near(chem, z, sides, xf, yf), near(scaled, z, side_scaled, xf, yf)):
                term = (m + m_near) * (u_near - u)
                flux = term if flux is None else flux + term
            out[tile, rows, :] = field[tile, rows, :] + flux


def y_faces(masks, block):
    faces = []
    for yf in (0, 7):
        parts = []
        for xf in range(4):
            held = jnp.zeros((8, LANES), F32)
            for z in range(SLABS):
                tile = block[8 * xf + yf, slab(z), :]
                held = jnp.where(masks["yc"] == z, turned(tile, (z - yf) * 16), held)
            parts.append(held)
        faces.append(jnp.concatenate(parts, 0))
    return faces


def add_y(masks, block, d, change):
    yf = 7 if d == 2 else 0
    where = masks["y_last" if d == 2 else "y_first"]
    for xf in range(4):
        for z in range(SLABS):
            spread = turned(change[8 * xf : 8 * xf + 8], (yf - z) * 16)
            tile = 8 * xf + yf
            block[tile, slab(z), :] = block[tile, slab(z), :] + jnp.where(where, spread, 0.0)


def add_z(block, d, change):
    row = TOP + 63 if d == 4 else TOP
    set_z_rows(block, row, z_rows(block, row) + change)


def y_halo(face, side, xf, z):
    place = 7 if side == 2 else 0
    return turned(face[part(xf), :], lax.rem((place - z) * 16 + LANES, LANES))


def x_halo(face, side, yf, z):
    place = 15 if side == 0 else 0
    spot = (yf & 1) * 8 + z
    return turned(face[part(yf >> 1), :], lax.rem(place - spot + LANES, LANES))


def group_in(stage, xf, pair):
    rows = [stage[4 * yc + pair, pl.ds(xf, 16, stride=4), :] for yc in range(8)]
    return jnp.concatenate(rows, 0).T


def group_out(stage, xf, pair, block):
    tile = 8 * xf + 2 * pair
    both = jnp.concatenate([block[tile, TOP : TOP + 64, :], block[tile + 1, TOP : TOP + 64, :]], 0).T
    for yc in range(8):
        stage[4 * yc + pair, pl.ds(xf, 16, stride=4), :] = both[16 * yc : 16 * yc + 16]


def place():
    size = lax.axis_size(AXES)
    minor = lax.axis_size("gy")
    me = lax.axis_index("gx") * minor + lax.axis_index("gy")
    upper, lower = lax.rem(me + 1, size), lax.rem(me + size - 1, size)

    def coordinates(device):
        return (device // minor, lax.rem(device, minor))

    return size, me, coordinates(upper), coordinates(lower)


def remote(source, target, send, receive, device):
    return pltpu.make_async_remote_copy(
        source, target, send, receive, device_id=device, device_id_type=MESH
    )


def own_kernel(
    c_hbm, links, owner, slot, stage, got, got_layers, got_marks,
    field, chem, scaled, side_mobility, pay, y_c, z_c, y_u, z_u, sent_c, sent_u, came_c, came_u, packed, marks, table, local, remote_face,
    load_sem, face_send, face_recv, block_send, block_recv, pack_send, pack_recv, lower_here,
):
    size, me, upper, lower = place()
    masks = masks_of()

    def load(b, xo):
        return pltpu.make_async_copy(c_hbm.at[b, xo], stage.at[b, :, eight(xo), :], load_sem.at[b, xo])

    @pl.loop(0, BLOCKS * SLABS)
    def _(i):
        load(i // SLABS, i % SLABS).start()

    barrier = pltpu.get_barrier_semaphore()
    pl.semaphore_signal(barrier, inc=1, device_id=lower, device_id_type=MESH)

    def link(b, d):
        return links[b, d]

    near_base = {2: 0, 3: 8, 4: 0, 5: 8}
    far_base = {2: 18, 3: 16, 4: 16, 5: 18}
    own_base = {2: 8, 3: 0, 4: 8, 5: 0}
    picks = {}
    for d in (2, 3, 4, 5):
        least, first, second = jnp.int32(BLOCKS), jnp.int32(BLOCKS - 1), jnp.int32(0)
        for b in range(BLOCKS):
            p = link(b, d)
            far = (p >= 0) & ((p >> 3) != me)
            least = jnp.where(far, jnp.minimum(least, p & 7), least)
            first = jnp.where(far, jnp.minimum(first, b), first)
            second = jnp.where(far, b, second)
        picks[d] = (first + own_base[d], second + own_base[d])
        for b in range(BLOCKS):
            p = link(b, d)
            far = far_base[d] + ((p & 7) > least).astype(jnp.int32)
            own, near = own_base[d] + b, near_base[d] + (p & 7)
            here = (p >> 3) == me
            table[b * 6 + d] = jnp.where(p < 0, own, jnp.where(here, near, far))
            local[b * 6 + d] = jnp.where((p >= 0) & here, near, own)
            remote_face[b * 6 + d] = jnp.where((p >= 0) & ~here, far, own)
    moving, mark_right, mark_left = jnp.int32(0), jnp.int32(0), jnp.int32(0)
    for b in range(BLOCKS):
        goes_right, goes_left = owner[b] == me + 1, owner[b] == me - 1
        moving = jnp.where(goes_right, b, moving)
        mark_right = jnp.where(goes_right, slot[b] + 1, mark_right)
        mark_left = jnp.where((owner[b] >= 0) & goes_left, slot[b] + 1, mark_left)
    marks[0] = jnp.full((8, LANES), mark_right, jnp.int32).astype(F32)
    marks[1] = jnp.full((8, LANES), mark_left, jnp.int32).astype(F32)

    def take_in(b, xf, pair, extra=None):
        both = group_in(stage.at[b], xf, pair)
        for h in range(2):
            tile, values = 8 * xf + 2 * pair + h, both[64 * h : 64 * h + 64]
            if extra is None:
                field[b, tile, TOP : TOP + 64, :] = values
                scaled[b, tile, TOP : TOP + 64, :] = mobility(values)
            else:
                pay[extra, tile] = values

    def take_blocks(start, end):
        @pl.loop(start, end)
        def _(b):
            @pl.loop(0, 4)
            def _(k):
                for q in range(4):
                    take_in(b, k, q)

    def block_copy(side, z):
        return remote(
            pay.at[side, :, eight(z), :], got.at[side, :, slab(z), :],
            block_send.at[side, z], block_recv.at[side, z], (upper, lower)[side],
        )

    has_upper, has_lower = me < size - 1, me > 0

    def hand_on(side, start, end):
        @pl.when((has_upper, has_lower)[side])
        def _():
            for z in range(start, end):
                block_copy(side, z).start()

    @pl.loop(0, BLOCKS * SLABS)
    def _(i):
        load(i // SLABS, i % SLABS).wait()

    @pl.loop(0, 4)
    def _(k):
        for q in range(4):
            take_in(moving, k, q, 0)

    pl.semaphore_wait(barrier, 1)
    pl.semaphore_signal(lower_here, inc=1, device_id=upper, device_id_type=MESH)
    hand_on(0, 0, AFTER[0])
    take_blocks(0, 1)

    @pl.loop(0, TILES)
    def _(t):
        pay[1, t] = field[0, t, TOP : TOP + 64, :]

    @pl.when(has_lower)
    def _():
        pl.semaphore_wait(lower_here, 1)

    hand_on(1, 0, AFTER[0])

    def hand_more(k):
        for side in range(2):
            hand_on(side, AFTER[k - 1], AFTER[k])

    take_blocks(1, 5)
    hand_more(1)
    take_blocks(5, BLOCKS)

    def faces_of(values, y_table, z_table):
        @pl.loop(0, BLOCKS)
        def _(b):
            z_table[b] = z_rows(values.at[b], TOP)
            z_table[BLOCKS + b] = z_rows(values.at[b], TOP + 63)
            y_table[b], y_table[BLOCKS + b] = y_faces(masks, values.at[b])

    faces_of(field, y_c, z_c)

    def fill(message, y_table, z_table):
        for side, (y_dir, z_dir) in enumerate(((2, 5), (3, 4))):
            for k in range(2):
                message[side, k] = y_table[picks[y_dir][k]]
                message[side, 2 + k] = z_table[picks[z_dir][k]]

    def face_copies(k, message, came):
        return [
            remote(message.at[side], came.at[side], face_send.at[k, side], face_recv.at[k, side], device)
            for side, device in enumerate((upper, lower))
        ]

    def take(came, y_table, z_table):
        for side in range(2):
            for k in range(2):
                y_table[16 + 2 * side + k] = came[side, k]
                z_table[16 + 2 * side + k] = came[side, 2 + k]

    def halo_of(values, y_table, b, z):
        rows = slab(z)
        open_high, open_low = link(b, 0) < 0, link(b, 1) < 0
        high = jnp.where(open_high, b, link(b, 0) & 7)
        low = jnp.where(open_low, b, link(b, 1) & 7)

        def halo(side, k):
            if side == 0:
                return jnp.where(open_high, values[b, 24 + k, rows, :], turned(values[high, k, rows, :], 15))
            if side == 1:
                return jnp.where(open_low, values[b, k, rows, :], turned(values[low, 24 + k, rows, :], -15))
            return y_halo(y_table.at[local[b * 6 + side]], side, k, z)

        return halo

    def set_z(values, z_table, b, scale=None):
        for row, d in ((TOP + 64, 4), (TOP - 1, 5)):
            layer = z_table[local[b * 6 + d]]
            set_z_rows(values.at[b], row, layer)
            if scale is not None:
                set_z_rows(scale.at[b], row, mobility(layer))

    fill(sent_c, y_c, z_c)

    @pl.when(me == 0)
    def _():
        pl.semaphore_wait(lower_here, 1)

    first_faces = face_copies(0, sent_c, came_c)
    for copy in first_faces:
        copy.start()
    hand_more(2)

    @pl.loop(0, BLOCKS)
    def _(b):
        set_z(field, z_c, b, scaled)

    def chemical_blocks(start, end):
        @pl.loop(start * (SLABS // STEP), end * (SLABS // STEP))
        def _(i):
            b = i // (SLABS // STEP)
            for q in range(STEP):
                z = i % (SLABS // STEP) * STEP + q
                chemical_slab(masks, field.at[b], chem.at[b], side_mobility.at[b], z, halo_of(field, y_c, b, z))

    chemical_blocks(0, 4)
    hand_more(3)
    chemical_blocks(4, BLOCKS)

    for copy in first_faces:
        copy.wait_recv()
    take(came_c, y_c, z_c)

    @pl.loop(0, BLOCKS)
    def _(b):
        for d in (2, 3):
            own = y_c[own_base[d] + b]
            add_y(masks, chem.at[b], d, -2.0 * (y_c[remote_face[b * 6 + d]] - own))
        for d in (4, 5):
            own = z_c[own_base[d] + b]
            add_z(chem.at[b], d, -2.0 * (z_c[remote_face[b * 6 + d]] - own))

    faces_of(chem, y_u, z_u)
    fill(sent_u, y_u, z_u)
    second_faces = face_copies(1, sent_u, came_u)
    for copy in second_faces:
        copy.start()
    hand_more(4)

    def pack(k, values, y_table, z_table):
        for side, b in ((0, moving), (1, 0)):
            for d in (2, 3):
                packed[side, k, d] = y_table[table[b * 6 + d]]
            for d in (4, 5):
                packed[side, k, d] = z_table[table[b * 6 + d]]


        @pl.loop(0, 4)
        def _(v):
            for side, b in ((0, moving), (1, 0)):
                for d in range(2):
                    closed = link(b, d) < 0
                    beside = jnp.where(closed, b, link(b, d) & 7)
                    inner, outer = (24, 0) if d == 0 else (0, 24)
                    place_in, place_out = (15, 0) if d == 0 else (0, 15)
                    mine, other = jnp.zeros((8, LANES), F32), jnp.zeros((8, LANES), F32)
                    for e in range(2):
                        for z in range(SLABS):
                            spot, k8 = 8 * e + z, 2 * v + e
                            there = masks["xc"] == spot
                            own = turned(values[b, inner + k8, slab(z), :], spot - place_in)
                            far = turned(values[beside, outer + k8, slab(z), :], spot - place_out)
                            mine, other = jnp.where(there, own, mine), jnp.where(there, far, other)
                    packed[side, k, d, eight(v), :] = jnp.where(closed, mine, other)

    pack(0, field, y_c, z_c)

    @pl.loop(0, BLOCKS)
    def _(b):
        set_z(chem, z_u, b)

    def advance_blocks(start, end):
        @pl.loop(start * (SLABS // STEP), end * (SLABS // STEP))
        def _(i):
            b = i // (SLABS // STEP)
            for q in range(STEP):
                z = i % (SLABS // STEP) * STEP + q
                advance_slab(
                    masks, field.at[b], chem.at[b], scaled.at[b], side_mobility.at[b], field.at[b], z,
                    halo_of(chem, y_u, b, z),
                )

    advance_blocks(0, SPLIT)
    hand_more(5)

    for copy in second_faces:
        copy.wait_recv()
    take(came_u, y_u, z_u)
    pack(1, chem, y_u, z_u)

    def pack_copies(side):
        device = (upper, lower)[side]
        return [
            remote(packed.at[side], got_layers.at[side], pack_send.at[0, side], pack_recv.at[0, side], device),
            remote(marks.at[side], got_marks.at[side], pack_send.at[1, side], pack_recv.at[1, side], device),
        ]

    for side in range(2):

        @pl.when((has_upper, has_lower)[side])
        def _(side=side):
            for copy in pack_copies(side):
                copy.start()

    advance_blocks(SPLIT, BLOCKS)

    def far_flux(field_table, chem_table, b, d):
        own, far = own_base[d] + b, remote_face[b * 6 + d]
        passing = mobility(field_table[own]) + mobility(field_table[far])
        return passing * (chem_table[far] - chem_table[own])

    @pl.loop(0, BLOCKS)
    def _(b):
        for d in (2, 3):
            add_y(masks, field.at[b], d, far_flux(y_c, y_u, b, d))
        for d in (4, 5):
            add_z(field.at[b], d, far_flux(z_c, z_u, b, d))

    @pl.loop(0, BLOCKS * 4)
    def _(i):
        b, k = i // 4, i % 4
        for q in range(4):
            group_out(stage.at[b], k, q, field.at[b])

    for side in range(2):

        @pl.when((has_upper, has_lower)[side])
        def _(side=side):
            for copy in pack_copies(side) + [block_copy(side, z) for z in range(SLABS)]:
                copy.wait_send()

        @pl.when((has_lower, has_upper)[side])
        def _(side=side):
            for copy in pack_copies(side) + [block_copy(side, z) for z in range(SLABS)]:
                copy.wait_recv()

    for copy in first_faces + second_faces:
        copy.wait_send()


def layout_kernel(
    stage, got, got_layers, got_marks, owner, slot, out,
    arrived, scaled, chem, stepped, side_mobility, final, zeros, keep_sem, zero_sem, new_sem,
):
    size, me, _, _ = place()
    masks = masks_of()

    def keep_copy(b, xo):
        return pltpu.make_async_copy(stage.at[b, :, 8 * xo : 8 * xo + 8, :], out.at[slot[b], xo], keep_sem.at[b, xo])

    def new_copy(side, xo):
        return pltpu.make_async_copy(
            final.at[side, :, 8 * xo : 8 * xo + 8, :], out.at[places[side] - 1, xo], new_sem.at[side, xo]
        )

    kept = jnp.int32(0)
    for b in range(BLOCKS):
        stays = owner[b] == me
        kept = kept + stays.astype(jnp.int32)

        @pl.when(stays)
        def _(b=b):
            for xo in range(SLABS):
                keep_copy(b, xo).start()

    places = [
        jnp.where(there, jnp.max(got_marks[side]).astype(jnp.int32), 0)
        for side, there in enumerate((me > 0, me < size - 1))
    ]
    count = kept
    for target in places:
        count = count + (target > 0).astype(jnp.int32)
    zeros[...] = jnp.zeros_like(zeros)
    for s in range(BLOCKS):

        @pl.when(s >= count)
        def _(s=s):
            pltpu.make_async_copy(zeros, out.at[s], zero_sem.at[s]).start()

    for side in range(2):

        @pl.when(places[side] > 0)
        def _(side=side):
            layers = got_layers.at[side]

            def halo_of(k, z):
                def halo(d, f):
                    return (x_halo if d < 2 else y_halo)(layers.at[k, d], d, f, z)

                return halo

            @pl.loop(0, SLABS)
            def _(z):
                rows = slab(z)
                for t in range(TILES):
                    values = got[side, t, rows, :]
                    arrived[t, rows, :] = values
                    scaled[t, rows, :] = mobility(values)

            for row, d in ((TOP + 64, 4), (TOP - 1, 5)):
                set_z_rows(arrived, row, layers[0, d])
                set_z_rows(scaled, row, mobility(layers[0, d]))
                set_z_rows(chem, row, layers[1, d])

            @pl.loop(0, SLABS // STEP)
            def _(i):
                for q in range(STEP):
                    z = i * STEP + q
                    chemical_slab(masks, arrived, chem, side_mobility, z, halo_of(0, z))

            @pl.loop(0, SLABS // STEP)
            def _(i):
                for q in range(STEP):
                    z = i * STEP + q
                    advance_slab(masks, arrived, chem, scaled, side_mobility, stepped, z, halo_of(1, z))

            @pl.loop(0, 4)
            def _(k):
                for q in range(4):
                    group_out(final.at[side], k, q, stepped)

            for xo in range(SLABS):
                new_copy(side, xo).start()

    for b in range(BLOCKS):

        @pl.when(owner[b] == me)
        def _(b=b):
            for xo in range(SLABS):
                keep_copy(b, xo).wait()

    for s in range(BLOCKS):

        @pl.when(s >= count)
        def _(s=s):
            pltpu.make_async_copy(zeros, out.at[s], zero_sem.at[s]).wait()

    for side in range(2):

        @pl.when(places[side] > 0)
        def _(side=side):
            for xo in range(SLABS):
                new_copy(side, xo).wait()


def per_device(concentration, neighbour, new_owner, new_slot):
    tiles = concentration.reshape(BLOCKS, SLABS, 8, 32, LANES).transpose(0, 1, 3, 2, 4)
    anywhere = pl.BlockSpec(memory_space=pl.ANY)
    scalars = pl.BlockSpec(memory_space=pltpu.SMEM)
    vector = pl.BlockSpec(memory_space=pltpu.VMEM)
    padded = (TILES, PITCH, LANES)
    plain = (TILES, 64, LANES)
    sides = (24, 64, LANES)
    tables = [pltpu.VMEM((20, *FACE), F32)] * 4
    dma = pltpu.SemaphoreType.DMA
    stage, got, got_layers, got_marks = pl.pallas_call(
        own_kernel,
        out_shape=[
            pltpu.VMEM((BLOCKS, *plain), F32),
            pltpu.VMEM((2, *padded), F32),
            pltpu.VMEM((2, 2, 6, *FACE), F32),
            pltpu.VMEM((2, 8, LANES), F32),
        ],
        in_specs=[anywhere, scalars, scalars, scalars],
        out_specs=[vector] * 4,
        scratch_shapes=[
            *[pltpu.VMEM((BLOCKS, *padded), F32)] * 3,
            pltpu.VMEM((BLOCKS, *sides), F32),
            pltpu.VMEM((2, *plain), F32),
            *tables,
            *[pltpu.VMEM((2, 4, *FACE), F32)] * 4,
            pltpu.VMEM((2, 2, 6, *FACE), F32),
            pltpu.VMEM((2, 8, LANES), F32),
            *[pltpu.SMEM((BLOCKS * 6,), jnp.int32)] * 3,
            dma((BLOCKS, SLABS)),
            dma((2, 2)),
            dma((2, 2)),
            dma((2, SLABS)),
            dma((2, SLABS)),
            dma((2, 2)),
            dma((2, 2)),
            pltpu.SemaphoreType.REGULAR,
        ],
        compiler_params=pltpu.CompilerParams(
            collective_id=0, has_side_effects=True, vmem_limit_bytes=48 << 20
        ),
    )(tiles, neighbour, new_owner, new_slot)
    out = pl.pallas_call(
        layout_kernel,
        out_shape=jax.ShapeDtypeStruct((BLOCKS, SLABS, 32, 8, LANES), F32),
        in_specs=[vector] * 4 + [scalars] * 2,
        out_specs=anywhere,
        scratch_shapes=[
            *[pltpu.VMEM(padded, F32)] * 4,
            pltpu.VMEM(sides, F32),
            pltpu.VMEM((2, *plain), F32),
            pltpu.VMEM((SLABS, 32, 8, LANES), F32),
            dma((BLOCKS, SLABS)),
            dma((BLOCKS,)),
            dma((2, SLABS)),
        ],
        compiler_params=pltpu.CompilerParams(vmem_limit_bytes=16 << 20),
    )(stage, got, got_layers, got_marks, new_owner, new_slot)
    return out.transpose(0, 1, 3, 2, 4).reshape(concentration.shape)


def solution(mesh):
    return jax.shard_map(
        per_device,
        mesh=mesh,
        in_specs=(P(AXES, None, None), P(AXES, None), P(AXES), P(AXES)),
        out_specs=P(AXES, None, None),
        check_vma=False,
    )
```

```python
import jax
import jax.numpy as jnp
from jax import lax
from jax.experimental import pallas as pl
from jax.experimental.pallas import tpu as pltpu
from jax.sharding import PartitionSpec as P

MESH = pl.DeviceIdType.MESH
AXES = ("gx", "gy")
BLOCKS = 8
LANES = 128
TILES = 32
SLABS = 8
TOP = 8
PITCH = 80
F32 = jnp.float32
FACE = (32, LANES)
AFTER = (2, 3, 4, 6, 8, 8)
STEP = 4
SPLIT = 5


def masks_of():
    lane = lax.broadcasted_iota(jnp.int32, (8, LANES), 1)
    xc, yc = lane & 15, lane >> 4
    return {
        "xc": xc,
        "yc": yc,
        "x_first": xc == 0,
        "x_last": xc == 15,
        "y_first": yc == 0,
        "y_last": yc == 7,
    }


def turned(tile, shift):
    if isinstance(shift, int):
        shift %= LANES
        if shift == 0:
            return tile
    return pltpu.roll(tile, shift, 1)


def mobility(values):
    square = values - values * values
    return 0.00075 + 0.04 * (square * square)


def slab(z, offset=0):
    if offset:
        return pl.ds(TOP + 8 * z + offset, 8)
    return pl.ds(TOP + 8 * z if isinstance(z, int) else pl.multiple_of(TOP + 8 * z, 8), 8)


def eight(z):
    return pl.ds(pl.multiple_of(8 * z, 8), 8)


def part(k):
    return pl.ds(8 * k, 8)


def rows_of(block):
    return block.reshape(TILES * PITCH, LANES)


def z_rows(block, row):
    return rows_of(block)[pl.ds(row, TILES, stride=PITCH), :]


def set_z_rows(block, row, values):
    rows_of(block)[pl.ds(row, TILES, stride=PITCH), :] = values


def shifted_sides(masks, block, z, halo):
    rows = slab(z)
    sides = []
    for yf in range(8):
        own = turned(block[yf, rows, :], -1)
        sides.append(jnp.where(masks["x_last"], halo(0, yf), own))
    for yf in range(8):
        own = turned(block[24 + yf, rows, :], 1)
        sides.append(jnp.where(masks["x_first"], halo(1, yf), own))
    for xf in range(4):
        own = turned(block[8 * xf, rows, :], -16)
        sides.append(jnp.where(masks["y_last"], halo(2, xf), own))
    for xf in range(4):
        own = turned(block[8 * xf + 7, rows, :], 16)
        sides.append(jnp.where(masks["y_first"], halo(3, xf), own))
    return sides


def near(block, z, sides, xf, yf):
    rows, tile = slab(z), 8 * xf + yf
    return (
        block[tile + 8, rows, :] if xf < 3 else sides[yf],
        block[tile - 8, rows, :] if xf > 0 else sides[8 + yf],
        block[tile + 1, rows, :] if yf < 7 else sides[16 + xf],
        block[tile - 1, rows, :] if yf > 0 else sides[20 + xf],
        block[tile, slab(z, 1), :],
        block[tile, slab(z, -1), :],
    )


def chemical_slab(masks, field, chem, side_mobility, z, halo):
    sides = shifted_sides(masks, field, z, halo)
    for k, values in enumerate(sides):
        side_mobility[k, eight(z), :] = mobility(values)
    rows = slab(z)
    for xf in range(4):
        for yf in range(8):
            tile = field[8 * xf + yf, rows, :]
            a, b, c, d, e, f = near(field, z, sides, xf, yf)
            total = ((a + b) + (c + d)) + (e + f)
            value = tile * (14.0 + tile * (4.0 * tile - 6.0)) - (total + total)
            chem[8 * xf + yf, rows, :] = value


def advance_slab(masks, field, chem, scaled, side_mobility, out, z, halo):
    sides = shifted_sides(masks, chem, z, halo)
    side_scaled = [side_mobility[k, eight(z), :] for k in range(24)]
    rows = slab(z)
    for xf in range(4):
        for yf in range(8):
            tile = 8 * xf + yf
            u, m = chem[tile, rows, :], scaled[tile, rows, :]
            flux = None
            for u_near, m_near in zip(near(chem, z, sides, xf, yf), near(scaled, z, side_scaled, xf, yf)):
                term = (m + m_near) * (u_near - u)
                flux = term if flux is None else flux + term
            out[tile, rows, :] = field[tile, rows, :] + flux


def y_faces(masks, block):
    faces = []
    for yf in (0, 7):
        parts = []
        for xf in range(4):
            held = jnp.zeros((8, LANES), F32)
            for z in range(SLABS):
                tile = block[8 * xf + yf, slab(z), :]
                held = jnp.where(masks["yc"] == z, turned(tile, (z - yf) * 16), held)
            parts.append(held)
        faces.append(jnp.concatenate(parts, 0))
    return faces


def add_y(masks, block, d, change):
    yf = 7 if d == 2 else 0
    where = masks["y_last" if d == 2 else "y_first"]
    for xf in range(4):
        for z in range(SLABS):
            spread = turned(change[8 * xf : 8 * xf + 8], (yf - z) * 16)
            tile = 8 * xf + yf
            block[tile, slab(z), :] = block[tile, slab(z), :] + jnp.where(where, spread, 0.0)


def add_z(block, d, change):
    row = TOP + 63 if d == 4 else TOP
    set_z_rows(block, row, z_rows(block, row) + change)


def y_halo(face, side, xf, z):
    place = 7 if side == 2 else 0
    return turned(face[part(xf), :], lax.rem((place - z) * 16 + LANES, LANES))


def x_halo(face, side, yf, z):
    place = 15 if side == 0 else 0
    spot = (yf & 1) * 8 + z
    return turned(face[part(yf >> 1), :], lax.rem(place - spot + LANES, LANES))


def group_in(stage, xf, pair):
    rows = [stage[4 * yc + pair, pl.ds(xf, 16, stride=4), :] for yc in range(8)]
    return jnp.concatenate(rows, 0).T


def group_out(stage, xf, pair, block):
    tile = 8 * xf + 2 * pair
    both = jnp.concatenate([block[tile, TOP : TOP + 64, :], block[tile + 1, TOP : TOP + 64, :]], 0).T
    for yc in range(8):
        stage[4 * yc + pair, pl.ds(xf, 16, stride=4), :] = both[16 * yc : 16 * yc + 16]


def place():
    size = lax.axis_size(AXES)
    minor = lax.axis_size("gy")
    me = lax.axis_index("gx") * minor + lax.axis_index("gy")
    upper, lower = lax.rem(me + 1, size), lax.rem(me + size - 1, size)

    def coordinates(device):
        return (device // minor, lax.rem(device, minor))

    return size, me, coordinates(upper), coordinates(lower)


def remote(source, target, send, receive, device):
    return pltpu.make_async_remote_copy(
        source, target, send, receive, device_id=device, device_id_type=MESH
    )


def own_kernel(
    c_hbm, links, owner, slot, stage, got, got_layers, got_marks,
    field, chem, scaled, side_mobility, pay, y_c, z_c, y_u, z_u, sent_c, sent_u, came_c, came_u, packed, marks, table, local, remote_face,
    load_sem, face_send, face_recv, block_send, block_recv, pack_send, pack_recv, lower_here,
):
    size, me, upper, lower = place()
    masks = masks_of()

    def load(b, xo):
        return pltpu.make_async_copy(c_hbm.at[b, xo], stage.at[b, :, eight(xo), :], load_sem.at[b, xo])

    @pl.loop(0, BLOCKS * SLABS)
    def _(i):
        load(i // SLABS, i % SLABS).start()

    barrier = pltpu.get_barrier_semaphore()
    pl.semaphore_signal(barrier, inc=1, device_id=lower, device_id_type=MESH)

    def link(b, d):
        return links[b, d]

    near_base = {2: 0, 3: 8, 4: 0, 5: 8}
    far_base = {2: 18, 3: 16, 4: 16, 5: 18}
    own_base = {2: 8, 3: 0, 4: 8, 5: 0}
    picks = {}
    for d in (2, 3, 4, 5):
        least, first, second = jnp.int32(BLOCKS), jnp.int32(BLOCKS - 1), jnp.int32(0)
        for b in range(BLOCKS):
            p = link(b, d)
            far = (p >= 0) & ((p >> 3) != me)
            least = jnp.where(far, jnp.minimum(least, p & 7), least)
            first = jnp.where(far, jnp.minimum(first, b), first)
            second = jnp.where(far, b, second)
        picks[d] = (first + own_base[d], second + own_base[d])
        for b in range(BLOCKS):
            p = link(b, d)
            far = far_base[d] + ((p & 7) > least).astype(jnp.int32)
            own, near = own_base[d] + b, near_base[d] + (p & 7)
            here = (p >> 3) == me
            table[b * 6 + d] = jnp.where(p < 0, own, jnp.where(here, near, far))
            local[b * 6 + d] = jnp.where((p >= 0) & here, near, own)
            remote_face[b * 6 + d] = jnp.where((p >= 0) & ~here, far, own)
    moving, mark_right, mark_left = jnp.int32(0), jnp.int32(0), jnp.int32(0)
    for b in range(BLOCKS):
        goes_right, goes_left = owner[b] == me + 1, owner[b] == me - 1
        moving = jnp.where(goes_right, b, moving)
        mark_right = jnp.where(goes_right, slot[b] + 1, mark_right)
        mark_left = jnp.where((owner[b] >= 0) & goes_left, slot[b] + 1, mark_left)
    marks[0] = jnp.full((8, LANES), mark_right, jnp.int32).astype(F32)
    marks[1] = jnp.full((8, LANES), mark_left, jnp.int32).astype(F32)

    def take_in(b, xf, pair, extra=None):
        both = group_in(stage.at[b], xf, pair)
        for h in range(2):
            tile, values = 8 * xf + 2 * pair + h, both[64 * h : 64 * h + 64]
            if extra is None:
                field[b, tile, TOP : TOP + 64, :] = values
                scaled[b, tile, TOP : TOP + 64, :] = mobility(values)
            else:
                pay[extra, tile] = values

    def take_blocks(start, end):
        @pl.loop(start, end)
        def _(b):
            @pl.loop(0, 4)
            def _(k):
                for q in range(4):
                    take_in(b, k, q)

    def block_copy(side, z):
        return remote(
            pay.at[side, :, eight(z), :], got.at[side, :, slab(z), :],
            block_send.at[side, z], block_recv.at[side, z], (upper, lower)[side],
        )

    has_upper, has_lower = me < size - 1, me > 0

    def hand_on(side, start, end):
        @pl.when((has_upper, has_lower)[side])
        def _():
            for z in range(start, end):
                block_copy(side, z).start()

    @pl.loop(0, BLOCKS * SLABS)
    def _(i):
        load(i // SLABS, i % SLABS).wait()

    @pl.loop(0, 4)
    def _(k):
        for q in range(4):
            take_in(moving, k, q, 0)

    pl.semaphore_wait(barrier, 1)
    pl.semaphore_signal(lower_here, inc=1, device_id=upper, device_id_type=MESH)
    hand_on(0, 0, AFTER[0])
    take_blocks(0, 1)

    @pl.loop(0, TILES)
    def _(t):
        pay[1, t] = field[0, t, TOP : TOP + 64, :]

    @pl.when(has_lower)
    def _():
        pl.semaphore_wait(lower_here, 1)

    hand_on(1, 0, AFTER[0])

    def hand_more(k):
        for side in range(2):
            hand_on(side, AFTER[k - 1], AFTER[k])

    take_blocks(1, 5)
    hand_more(1)
    take_blocks(5, BLOCKS)

    def faces_of(values, y_table, z_table):
        @pl.loop(0, BLOCKS)
        def _(b):
            z_table[b] = z_rows(values.at[b], TOP)
            z_table[BLOCKS + b] = z_rows(values.at[b], TOP + 63)
            y_table[b], y_table[BLOCKS + b] = y_faces(masks, values.at[b])

    faces_of(field, y_c, z_c)

    def fill(message, y_table, z_table):
        for side, (y_dir, z_dir) in enumerate(((2, 5), (3, 4))):
            for k in range(2):
                message[side, k] = y_table[picks[y_dir][k]]
                message[side, 2 + k] = z_table[picks[z_dir][k]]

    def face_copies(k, message, came):
        return [
            remote(message.at[side], came.at[side], face_send.at[k, side], face_recv.at[k, side], device)
            for side, device in enumerate((upper, lower))
        ]

    def take(came, y_table, z_table):
        for side in range(2):
            for k in range(2):
                y_table[16 + 2 * side + k] = came[side, k]
                z_table[16 + 2 * side + k] = came[side, 2 + k]

    def halo_of(values, y_table, b, z):
        rows = slab(z)
        open_high, open_low = link(b, 0) < 0, link(b, 1) < 0
        high = jnp.where(open_high, b, link(b, 0) & 7)
        low = jnp.where(open_low, b, link(b, 1) & 7)

        def halo(side, k):
            if side == 0:
                return jnp.where(open_high, values[b, 24 + k, rows, :], turned(values[high, k, rows, :], 15))
            if side == 1:
                return jnp.where(open_low, values[b, k, rows, :], turned(values[low, 24 + k, rows, :], -15))
            return y_halo(y_table.at[local[b * 6 + side]], side, k, z)

        return halo

    def set_z(values, z_table, b, scale=None):
        for row, d in ((TOP + 64, 4), (TOP - 1, 5)):
            layer = z_table[local[b * 6 + d]]
            set_z_rows(values.at[b], row, layer)
            if scale is not None:
                set_z_rows(scale.at[b], row, mobility(layer))

    fill(sent_c, y_c, z_c)

    @pl.when(me == 0)
    def _():
        pl.semaphore_wait(lower_here, 1)

    first_faces = face_copies(0, sent_c, came_c)
    for copy in first_faces:
        copy.start()
    hand_more(2)

    @pl.loop(0, BLOCKS)
    def _(b):
        set_z(field, z_c, b, scaled)

    def chemical_blocks(start, end):
        @pl.loop(start * (SLABS // STEP), end * (SLABS // STEP))
        def _(i):
            b = i // (SLABS // STEP)
            for q in range(STEP):
                z = i % (SLABS // STEP) * STEP + q
                chemical_slab(masks, field.at[b], chem.at[b], side_mobility.at[b], z, halo_of(field, y_c, b, z))

    chemical_blocks(0, 4)
    hand_more(3)
    chemical_blocks(4, BLOCKS)

    for copy in first_faces:
        copy.wait_recv()
    take(came_c, y_c, z_c)

    @pl.loop(0, BLOCKS)
    def _(b):
        for d in (2, 3):
            own = y_c[own_base[d] + b]
            add_y(masks, chem.at[b], d, -2.0 * (y_c[remote_face[b * 6 + d]] - own))
        for d in (4, 5):
            own = z_c[own_base[d] + b]
            add_z(chem.at[b], d, -2.0 * (z_c[remote_face[b * 6 + d]] - own))

    faces_of(chem, y_u, z_u)
    fill(sent_u, y_u, z_u)
    second_faces = face_copies(1, sent_u, came_u)
    for copy in second_faces:
        copy.start()
    hand_more(4)

    def pack(k, values, y_table, z_table):
        for side, b in ((0, moving), (1, 0)):
            for d in (2, 3):
                packed[side, k, d] = y_table[table[b * 6 + d]]
            for d in (4, 5):
                packed[side, k, d] = z_table[table[b * 6 + d]]


        @pl.loop(0, 4)
        def _(v):
            for side, b in ((0, moving), (1, 0)):
                for d in range(2):
                    closed = link(b, d) < 0
                    beside = jnp.where(closed, b, link(b, d) & 7)
                    inner, outer = (24, 0) if d == 0 else (0, 24)
                    place_in, place_out = (15, 0) if d == 0 else (0, 15)
                    mine, other = jnp.zeros((8, LANES), F32), jnp.zeros((8, LANES), F32)
                    for e in range(2):
                        for z in range(SLABS):
                            spot, k8 = 8 * e + z, 2 * v + e
                            there = masks["xc"] == spot
                            own = turned(values[b, inner + k8, slab(z), :], spot - place_in)
                            far = turned(values[beside, outer + k8, slab(z), :], spot - place_out)
                            mine, other = jnp.where(there, own, mine), jnp.where(there, far, other)
                    packed[side, k, d, eight(v), :] = jnp.where(closed, mine, other)

    pack(0, field, y_c, z_c)

    @pl.loop(0, BLOCKS)
    def _(b):
        set_z(chem, z_u, b)

    def advance_blocks(start, end):
        @pl.loop(start * (SLABS // STEP), end * (SLABS // STEP))
        def _(i):
            b = i // (SLABS // STEP)
            for q in range(STEP):
                z = i % (SLABS // STEP) * STEP + q
                advance_slab(
                    masks, field.at[b], chem.at[b], scaled.at[b], side_mobility.at[b], field.at[b], z,
                    halo_of(chem, y_u, b, z),
                )

    advance_blocks(0, SPLIT)
    hand_more(5)

    for copy in second_faces:
        copy.wait_recv()
    take(came_u, y_u, z_u)
    pack(1, chem, y_u, z_u)

    def pack_copies(side):
        device = (upper, lower)[side]
        return [
            remote(packed.at[side], got_layers.at[side], pack_send.at[0, side], pack_recv.at[0, side], device),
            remote(marks.at[side], got_marks.at[side], pack_send.at[1, side], pack_recv.at[1, side], device),
        ]

    for side in range(2):

        @pl.when((has_upper, has_lower)[side])
        def _(side=side):
            for copy in pack_copies(side):
                copy.start()

    advance_blocks(SPLIT, BLOCKS)

    def far_flux(field_table, chem_table, b, d):
        own, far = own_base[d] + b, remote_face[b * 6 + d]
        passing = mobility(field_table[own]) + mobility(field_table[far])
        return passing * (chem_table[far] - chem_table[own])

    @pl.loop(0, BLOCKS)
    def _(b):
        for d in (2, 3):
            add_y(masks, field.at[b], d, far_flux(y_c, y_u, b, d))
        for d in (4, 5):
            add_z(field.at[b], d, far_flux(z_c, z_u, b, d))

    @pl.loop(0, BLOCKS * 4)
    def _(i):
        b, k = i // 4, i % 4
        for q in range(4):
            group_out(stage.at[b], k, q, field.at[b])

    for side in range(2):

        @pl.when((has_upper, has_lower)[side])
        def _(side=side):
            for copy in pack_copies(side) + [block_copy(side, z) for z in range(SLABS)]:
                copy.wait_send()

        @pl.when((has_lower, has_upper)[side])
        def _(side=side):
            for copy in pack_copies(side) + [block_copy(side, z) for z in range(SLABS)]:
                copy.wait_recv()

    for copy in first_faces + second_faces:
        copy.wait_send()


def layout_kernel(
    stage, got, got_layers, got_marks, owner, slot, out,
    arrived, scaled, chem, stepped, side_mobility, final, zeros, keep_sem, zero_sem, new_sem,
):
    size, me, _, _ = place()
    masks = masks_of()

    def keep_copy(b, xo):
        return pltpu.make_async_copy(stage.at[b, :, 8 * xo : 8 * xo + 8, :], out.at[slot[b], xo], keep_sem.at[b, xo])

    def new_copy(side, xo):
        return pltpu.make_async_copy(
            final.at[side, :, 8 * xo : 8 * xo + 8, :], out.at[places[side] - 1, xo], new_sem.at[side, xo]
        )

    kept = jnp.int32(0)
    for b in range(BLOCKS):
        stays = owner[b] == me
        kept = kept + stays.astype(jnp.int32)

        @pl.when(stays)
        def _(b=b):
            for xo in range(SLABS):
                keep_copy(b, xo).start()

    places = [
        jnp.where(there, jnp.max(got_marks[side]).astype(jnp.int32), 0)
        for side, there in enumerate((me > 0, me < size - 1))
    ]
    count = kept
    for target in places:
        count = count + (target > 0).astype(jnp.int32)
    zeros[...] = jnp.zeros_like(zeros)
    for s in range(BLOCKS):

        @pl.when(s >= count)
        def _(s=s):
            pltpu.make_async_copy(zeros, out.at[s], zero_sem.at[s]).start()

    for side in range(2):

        @pl.when(places[side] > 0)
        def _(side=side):
            layers = got_layers.at[side]

            def halo_of(k, z):
                def halo(d, f):
                    return (x_halo if d < 2 else y_halo)(layers.at[k, d], d, f, z)

                return halo

            @pl.loop(0, SLABS)
            def _(z):
                rows = slab(z)
                for t in range(TILES):
                    values = got[side, t, rows, :]
                    arrived[t, rows, :] = values
                    scaled[t, rows, :] = mobility(values)

            for row, d in ((TOP + 64, 4), (TOP - 1, 5)):
                set_z_rows(arrived, row, layers[0, d])
                set_z_rows(scaled, row, mobility(layers[0, d]))
                set_z_rows(chem, row, layers[1, d])

            @pl.loop(0, SLABS // STEP)
            def _(i):
                for q in range(STEP):
                    z = i * STEP + q
                    chemical_slab(masks, arrived, chem, side_mobility, z, halo_of(0, z))

            @pl.loop(0, SLABS // STEP)
            def _(i):
                for q in range(STEP):
                    z = i * STEP + q
                    advance_slab(masks, arrived, chem, scaled, side_mobility, stepped, z, halo_of(1, z))

            @pl.loop(0, 4)
            def _(k):
                for q in range(4):
                    group_out(final.at[side], k, q, stepped)

            for xo in range(SLABS):
                new_copy(side, xo).start()

    for b in range(BLOCKS):

        @pl.when(owner[b] == me)
        def _(b=b):
            for xo in range(SLABS):
                keep_copy(b, xo).wait()

    for s in range(BLOCKS):

        @pl.when(s >= count)
        def _(s=s):
            pltpu.make_async_copy(zeros, out.at[s], zero_sem.at[s]).wait()

    for side in range(2):

        @pl.when(places[side] > 0)
        def _(side=side):
            for xo in range(SLABS):
                new_copy(side, xo).wait()


def per_device(concentration, neighbour, new_owner, new_slot):
    tiles = concentration.reshape(BLOCKS, SLABS, 8, 32, LANES).transpose(0, 1, 3, 2, 4)
    anywhere = pl.BlockSpec(memory_space=pl.ANY)
    scalars = pl.BlockSpec(memory_space=pltpu.SMEM)
    vector = pl.BlockSpec(memory_space=pltpu.VMEM)
    padded = (TILES, PITCH, LANES)
    plain = (TILES, 64, LANES)
    sides = (24, 64, LANES)
    tables = [pltpu.VMEM((20, *FACE), F32)] * 4
    dma = pltpu.SemaphoreType.DMA
    stage, got, got_layers, got_marks = pl.pallas_call(
        own_kernel,
        out_shape=[
            pltpu.VMEM((BLOCKS, *plain), F32),
            pltpu.VMEM((2, *padded), F32),
            pltpu.VMEM((2, 2, 6, *FACE), F32),
            pltpu.VMEM((2, 8, LANES), F32),
        ],
        in_specs=[anywhere, scalars, scalars, scalars],
        out_specs=[vector] * 4,
        scratch_shapes=[
            *[pltpu.VMEM((BLOCKS, *padded), F32)] * 3,
            pltpu.VMEM((BLOCKS, *sides), F32),
            pltpu.VMEM((2, *plain), F32),
            *tables,
            *[pltpu.VMEM((2, 4, *FACE), F32)] * 4,
            pltpu.VMEM((2, 2, 6, *FACE), F32),
            pltpu.VMEM((2, 8, LANES), F32),
            *[pltpu.SMEM((BLOCKS * 6,), jnp.int32)] * 3,
            dma((BLOCKS, SLABS)),
            dma((2, 2)),
            dma((2, 2)),
            dma((2, SLABS)),
            dma((2, SLABS)),
            dma((2, 2)),
            dma((2, 2)),
            pltpu.SemaphoreType.REGULAR,
        ],
        compiler_params=pltpu.CompilerParams(
            collective_id=0, has_side_effects=True, vmem_limit_bytes=48 << 20
        ),
    )(tiles, neighbour, new_owner, new_slot)
    out = pl.pallas_call(
        layout_kernel,
        out_shape=jax.ShapeDtypeStruct((BLOCKS, SLABS, 32, 8, LANES), F32),
        in_specs=[vector] * 4 + [scalars] * 2,
        out_specs=anywhere,
        scratch_shapes=[
            *[pltpu.VMEM(padded, F32)] * 4,
            pltpu.VMEM(sides, F32),
            pltpu.VMEM((2, *plain), F32),
            pltpu.VMEM((SLABS, 32, 8, LANES), F32),
            dma((BLOCKS, SLABS)),
            dma((BLOCKS,)),
            dma((2, SLABS)),
        ],
        compiler_params=pltpu.CompilerParams(vmem_limit_bytes=16 << 20),
    )(stage, got, got_layers, got_marks, new_owner, new_slot)
    return out.transpose(0, 1, 3, 2, 4).reshape(concentration.shape)


def solution(mesh):
    return jax.shard_map(
        per_device,
        mesh=mesh,
        in_specs=(P(AXES, None, None), P(AXES, None), P(AXES), P(AXES)),
        out_specs=P(AXES, None, None),
        check_vma=False,
    )
```
